32 devices in a mesh: node: 8 (over z, y), local: 4 (over x, core).
Axes of the slice: x: 2, y: 2, z: 4, core: 2. Of those that a mesh axis runs over, the one named last changes fastest.
Arguments:
- tokens: bfloat16 [4096, 2048], P(('node', 'local')), may hold values from -6 to 6
- group_choice: int32 [4096, 4], P(('node', 'local')), may hold values from 0 to 7, as said below
- members: int32 [4096, 8], P(('node', 'local')), may hold values from 0 to 3, as said below
- route_weight: float32 [4096, 8], P(('node', 'local')), may hold values from 0.1 to 1
- expert_home: int32 [32], replicated, may hold values from 0 to 31, as said below
- expert_gate: bfloat16 [32, 2048, 768], P(('node', 'local')), may hold values from -0.125 to 0.125
- expert_up: bfloat16 [32, 2048, 768], P(('node', 'local')), may hold values from -0.125 to 0.125
- expert_down: bfloat16 [32, 768, 2048], P(('node', 'local')), may hold values from -0.21875 to 0.21875
- shared_gate: bfloat16 [2048, 1024], P(None, 'local'), may hold values from -0.125 to 0.125
- shared_up: bfloat16 [2048, 1024], P(None, 'local'), may hold values from -0.125 to 0.125
- shared_down: bfloat16 [1024, 2048], P('local'), may hold values from -0.1875 to 0.1875
Outputs:
- layer_out: bfloat16 [4096, 2048], P(('node', 'local'))
The draws below stay inside these ranges and needn't reach their ends.
Inputs may be any that keep to these rules, and one draw needn't show every extreme that they name: `group_choice`: each row names 4 different groups. `members`: entries 2j and 2j + 1 of a row differ. `expert_home`: A permutation; the experts of each group (consecutive blocks of 4) lie on the devices with indices in that same block.
All inputs are finite; a program needn't handle non-finite values.
Results may differ from the reference program's by a relative error of at most 0.0056.
Values may be sent and summed in bfloat16 or wider, within the bound.
No kernel may reach another device: no remote copies, remote signals or barrier semaphores. Data moves between devices by JAX's collectives and lax.ppermute only.
A program may use at most 128 MiB of HBM per device.

```python
import jax
import jax.numpy as jnp
from jax import lax

D = 2048
FF = 768
TOP = 8
GROUPS = 8
GROUP_TOP = 4
SHARED_FF = 1024
TOK_DEV = 128
EXPERTS = 32
TOKENS = 4096
CAP = 64
N_NODE = 8
N_LOCAL = 4


def draw_group_choice(key, part):
    key = jax.random.fold_in(key, 11)
    scores = jax.random.randint(key, (TOKENS, GROUPS), 0, 1 << 20) * GROUPS + jnp.arange(GROUPS, dtype=jnp.int32)[None, :]
    ranked = jnp.argsort(scores, axis=1, stable=True)
    return ranked[:, :GROUP_TOP].astype(jnp.int32)


def draw_members(key, part):
    key = jax.random.fold_in(key, 23)
    key_one, key_two, key_three = jax.random.split(key, 3)
    per_group = EXPERTS // GROUPS
    left_pick = jax.random.randint(key_one, (TOKENS, GROUP_TOP), 0, per_group)
    right_pick = jax.random.randint(key_two, (TOKENS, GROUP_TOP), 0, per_group)
    first_pick = left_pick * right_pick // per_group
    offset = jax.random.randint(key_three, (TOKENS, GROUP_TOP), 1, per_group)
    second_pick = (first_pick + offset) % per_group
    return jnp.stack([first_pick, second_pick], axis=-1).reshape(TOKENS, TOP).astype(jnp.int32)


def draw_expert_home(key, part):
    key = jax.random.fold_in(key, 37)
    per_group = EXPERTS // GROUPS
    scores = jax.random.randint(key, (GROUPS, per_group), 0, 1 << 20) * per_group + jnp.arange(per_group, dtype=jnp.int32)[None, :]
    shuffled = jnp.argsort(scores, axis=1, stable=True).astype(jnp.int32)
    homes = jnp.arange(GROUPS, dtype=jnp.int32)[:, None] * per_group + shuffled
    return homes.reshape(EXPERTS).astype(jnp.int32)


def block_scale(own_key, dims, cuts, low, high):
    gain = 1.0
    for dim, blocks in cuts:
        heights = jax.random.uniform(jax.random.fold_in(jax.random.fold_in(own_key, 6), dim), (blocks,), jnp.float32, low / len(cuts), high / len(cuts))
        gain = gain * jnp.repeat(jnp.exp(heights), dims[dim] // blocks).reshape((-1,) + (1,) * (len(dims) - 1 - dim))
    return gain


def bell_draw(key, extent, spread, bound, shards=(), kind=jnp.bfloat16):
    values = jax.random.normal(key, extent, jnp.float32) * spread
    if len(shards) > 0:
        values = block_scale(key, extent, shards, -0.22, 0.18) * values
    return jnp.clip(values, min=-bound, max=bound).astype(kind)


def setup_inputs(seed: int = 0) -> dict:
    key_list = jax.random.split(jax.random.key(seed), 12)
    tokens = bell_draw(key_list[0], (TOKENS, D), 1.0, 6.0, ((0, 32),))
    group_choice = draw_group_choice(jax.random.fold_in(key_list[11], 71), 0)
    members = draw_members(jax.random.fold_in(key_list[11], 71), 0)
    route_weight = jnp.clip(0.1 + 0.9 * jax.random.uniform(key_list[3], (TOKENS, TOP), jnp.float32) ** block_scale(key_list[3], (TOKENS, TOP), ((0, 32),), -0.2, 0.2), 0.1, 1.0)
    expert_home = draw_expert_home(jax.random.fold_in(key_list[11], 71), 0)
    expert_gate = bell_draw(key_list[5], (EXPERTS, D, FF), D ** -0.5, 0.125, ((0, 32),))
    expert_up = bell_draw(key_list[6], (EXPERTS, D, FF), D ** -0.5, 0.125, ((0, 32),))
    expert_down = bell_draw(key_list[7], (EXPERTS, FF, D), FF ** -0.5, 0.21875, ((0, 32),))
    shared_gate = bell_draw(key_list[8], (D, SHARED_FF), D ** -0.5, 0.125, ((1, 4),))
    shared_up = bell_draw(key_list[9], (D, SHARED_FF), D ** -0.5, 0.125, ((1, 4),))
    shared_down = bell_draw(key_list[10], (SHARED_FF, D), SHARED_FF ** -0.5, 0.1875, ((0, 4),))
    return dict(tokens=tokens, group_choice=group_choice, members=members, route_weight=route_weight, expert_home=expert_home, expert_gate=expert_gate, expert_up=expert_up, expert_down=expert_down, shared_gate=shared_gate, shared_up=shared_up, shared_down=shared_down)


def reference(tokens, group_choice, members, route_weight, expert_home, expert_gate, expert_up, expert_down, shared_gate, shared_up, shared_down):
    device_count = N_NODE * N_LOCAL
    per_group = EXPERTS // GROUPS
    chosen = jnp.repeat(group_choice, 2, axis=1) * per_group + members
    onehot = (chosen[:, :, None] == jnp.arange(EXPERTS, dtype=jnp.int32)[None, None, :]).astype(jnp.int32)
    target = jnp.sum(onehot * expert_home[None, None, :], axis=-1).astype(jnp.int32)
    blocks = onehot.reshape(device_count, TOK_DEV * TOP, EXPERTS)
    before = jnp.cumsum(blocks, axis=1) - blocks
    position = jnp.sum(before * blocks, axis=-1).reshape(TOKENS, TOP).astype(jnp.int32)
    source = (jnp.arange(TOKENS, dtype=jnp.int32) // TOK_DEV)[:, None]
    keep_mask = position < CAP
    column = jnp.where(keep_mask, source * CAP + position, device_count * CAP).astype(jnp.int32)
    token_id = jnp.broadcast_to(jnp.arange(TOKENS, dtype=jnp.int32)[:, None], (TOKENS, TOP))
    row_table = jnp.full((device_count, device_count * CAP), TOKENS, jnp.int32).at[target, column].set(token_id, mode="drop")
    weight_table = jnp.zeros((device_count, device_count * CAP), route_weight.dtype).at[target, column].set(route_weight, mode="drop")
    padded = jnp.concatenate([tokens, jnp.zeros((1, D), tokens.dtype)], axis=0)

    def expert_step(running, inputs):
        table_row, weight_row, local_gate, local_up, local_down = inputs
        row_block = padded[table_row]
        gate_part = jnp.dot(row_block, local_gate, preferred_element_type=jnp.float32)
        up_part = jnp.dot(row_block, local_up, preferred_element_type=jnp.float32)
        hidden = (jax.nn.silu(gate_part) * up_part).astype(jnp.bfloat16)
        result = jnp.dot(hidden, local_down, preferred_element_type=jnp.float32).astype(jnp.bfloat16)
        running = running.at[table_row].add(weight_row[:, None] * result.astype(running.dtype), mode="drop")
        return running, None

    running, _ = lax.scan(expert_step, jnp.zeros((TOKENS, D), jnp.float32), (row_table, weight_table, expert_gate, expert_up, expert_down))
    shared_hidden = (jax.nn.silu(jnp.dot(tokens, shared_gate, preferred_element_type=jnp.float32)) * jnp.dot(tokens, shared_up, preferred_element_type=jnp.float32)).astype(jnp.bfloat16)
    shared_part = jnp.dot(shared_hidden, shared_down, preferred_element_type=jnp.float32)
    return (running + shared_part).astype(jnp.bfloat16)
```

```python
import functools

import jax
import jax.numpy as jnp
from jax import lax
from jax.experimental import pallas as pl
from jax.experimental.pallas import tpu as pltpu
from jax.sharding import PartitionSpec as P

GROUPS = 8
AXES = ("node", "local")
F32 = jnp.float32
BF16 = jnp.bfloat16

Z_COUNT = 4


def permutation(move):
    pairs = []
    for z in range(Z_COUNT):
        for y in range(2):
            for x in range(2):
                for core in range(2):
                    to_z, to_y, to_x, to_core = move(z, y, x, core)
                    pairs.append(
                        (
                            ((z * 2 + y) * 2 + x) * 2 + core,
                            (((to_z % Z_COUNT) * 2 + to_y) * 2 + to_x) * 2 + to_core,
                        )
                    )
    return pairs


CORE = permutation(lambda z, y, x, core: (z, y, x, 1 - core))
ALONG_X = permutation(lambda z, y, x, core: (z, y, 1 - x, core))
ALONG_Y = permutation(lambda z, y, x, core: (z, 1 - y, x, core))
Z_UP = permutation(lambda z, y, x, core: (z + 1, y, x, core))
Z_DOWN = permutation(lambda z, y, x, core: (z - 1, y, x, core))


def send(value, pairs):
    return lax.ppermute(value, AXES, pairs)


def join(*values, axis=1):
    return jnp.concatenate(values, axis=axis)


def barrier(*values):
    return lax.optimization_barrier(values)


def expert_kernel(
    source_count,
    shared_count,
    capacity,
    weight_ref,
    own_ref,
    other_ref,
    gate_ref,
    up_ref,
    down_ref,
    *rest,
):
    if shared_count:
        sgate_ref, sup_ref, sdown_ref = rest[:3]
        rest = rest[3:]
    own_out, other_out, rows, hidden, answers = rest[:5]
    tokens = own_ref.shape[2]
    width = own_ref.shape[3]
    inner = gate_ref.shape[2]
    weights = weight_ref[...]
    hits = (weights > 0.0).astype(BF16)
    earlier = (
        lax.broadcasted_iota(jnp.int32, (tokens, tokens), 0)
        < lax.broadcasted_iota(jnp.int32, (tokens, tokens), 1)
    ).astype(BF16)
    place = jnp.dot(hits, earlier, preferred_element_type=F32).astype(jnp.int32)
    slots = lax.broadcasted_iota(jnp.int32, (capacity, tokens), 0)
    source_of = []
    for index in range(source_count):
        chunk, core, block = index // 8, index // 4 % 2, index % 4
        source_of.append((own_ref, own_out) if core == 0 else (other_ref, other_out))
        chosen = (place[index : index + 1] == slots) & (weights[index : index + 1] > 0.0)
        block_tokens = source_of[index][0][chunk, block]
        rows[pl.ds(index * capacity, capacity)] = jnp.dot(
            chosen.astype(BF16), block_tokens, preferred_element_type=F32
        ).astype(BF16)

    tile = 256
    group = 8 * capacity

    def up_step(step, carry):
        columns = pl.ds(pl.multiple_of(step * tile, tile), tile)
        for start in range(0, source_count * capacity, group):
            block_rows = rows[pl.ds(start, group)]
            gate_part = jnp.dot(block_rows, gate_ref[0, :, columns], preferred_element_type=F32)
            up_part = jnp.dot(block_rows, up_ref[0, :, columns], preferred_element_type=F32)
            hidden[pl.ds(start, group), columns] = (
                gate_part / (1.0 + jnp.exp(-gate_part)) * up_part
            ).astype(BF16)
        return carry

    lax.fori_loop(0, inner // tile, up_step, 0)

    shared_hidden = None
    if shared_count:
        shared_rows = jnp.concatenate(
            [own_ref[0, 0], own_ref[0, 1], other_ref[0, 0], other_ref[0, 1]], axis=0
        )
        gate_part = jnp.dot(shared_rows, sgate_ref[...], preferred_element_type=F32)
        up_part = jnp.dot(shared_rows, sup_ref[...], preferred_element_type=F32)
        rest[5][...] = (gate_part / (1.0 + jnp.exp(-gate_part)) * up_part).astype(BF16)

    out_tile = 512

    def down_step(step, carry):
        columns = pl.ds(pl.multiple_of(step * out_tile, out_tile), out_tile)
        for start in range(0, source_count * capacity, group):
            answers[pl.ds(start, group)] = jnp.dot(
                hidden[pl.ds(start, group)],
                down_ref[0, :, columns],
                preferred_element_type=F32,
            ).astype(BF16)
        for index in range(source_count):
            chunk, core, block = index // 8, index // 4 % 2, index % 4
            weight_row = weights[index : index + 1]
            chosen = (place[index : index + 1] == slots) & (weight_row > 0.0)
            spread = jnp.where(chosen, jnp.broadcast_to(weight_row, chosen.shape), 0.0)
            high = spread.astype(BF16)
            low = (spread - high.astype(F32)).astype(BF16)
            answer = answers[pl.ds(index * capacity, capacity)]
            total = lax.dot_general(
                jnp.concatenate([high, low], axis=0),
                jnp.concatenate([answer, answer], axis=0),
                (((0,), (0,)), ((), ())),
                preferred_element_type=F32,
            )
            if shared_count and chunk == 0 and block < 2:
                total = total + jnp.dot(
                    rest[5][pl.ds((core * 2 + block) * tokens, tokens)],
                    sdown_ref[:, columns],
                    preferred_element_type=F32,
                )
            source_of[index][1][chunk, block, :, columns] = total.astype(BF16)
        return carry

    lax.fori_loop(0, width // out_tile, down_step, 0)


def expert_chunk(weights, own, other, expert_weights, shared_weights, capacity):
    chunks, _, tokens, width = own.shape
    source_count = chunks * 8
    inner = expert_weights[0].shape[2]
    shared_width = shared_weights[0].shape[1] if shared_weights else 0
    scratch = [
        pltpu.VMEM((source_count * capacity, width), BF16),
        pltpu.VMEM((source_count * capacity, inner), BF16),
        pltpu.VMEM((source_count * capacity, 512), BF16),
    ]
    if shared_weights:
        scratch.append(pltpu.VMEM((4 * tokens, shared_width), BF16))
    flops = 2 * source_count * capacity * (3 * width * inner + 2 * tokens * width)
    operands = (weights, own, other, *expert_weights, *shared_weights)
    return pl.pallas_call(
        functools.partial(expert_kernel, source_count, len(shared_weights), capacity),
        out_shape=[jax.ShapeDtypeStruct(own.shape, BF16)] * 2,
        in_specs=[pl.BlockSpec(memory_space=pltpu.VMEM)] * len(operands),
        out_specs=[pl.BlockSpec(memory_space=pltpu.VMEM)] * 2,
        scratch_shapes=scratch,
        cost_estimate=pl.CostEstimate(
            flops=flops, bytes_accessed=3 * width * inner * 2 + 8 * own.size, transcendentals=0
        ),
        compiler_params=pltpu.CompilerParams(vmem_limit_bytes=56 * 1024 * 1024),
    )(*operands)


def route_table(group_choice, members, route_weight, expert_home, capacity):
    tok_rows = members.shape[0]
    experts_all = expert_home.shape[0]
    per_group = experts_all // GROUPS
    chosen = jnp.repeat(group_choice, 2, axis=1) * per_group + members
    ids = jnp.arange(experts_all, dtype=jnp.int32)
    target = jnp.sum(
        jnp.where(chosen[:, :, None] == ids[None, None, :], expert_home[None, None, :], 0), axis=-1
    )
    table = jnp.sum(
        jnp.where(target[:, :, None] == ids[None, None, :], route_weight[:, :, None], 0.0), axis=1
    )
    hits = (table > 0.0).astype(BF16)
    earlier = (
        lax.broadcasted_iota(jnp.int32, (tok_rows, tok_rows), 0)
        > lax.broadcasted_iota(jnp.int32, (tok_rows, tok_rows), 1)
    ).astype(BF16)
    place = jnp.dot(earlier, hits, preferred_element_type=F32)
    table = jnp.where(place < capacity, table, 0.0)
    return table.T


def block_device(
    tokens,
    group_choice,
    members,
    route_weight,
    expert_home,
    expert_gate,
    expert_up,
    expert_down,
    shared_gate,
    shared_up,
    shared_down,
):
    tok_rows, width = tokens.shape
    experts_all = expert_home.shape[0]
    capacity = 2 * tok_rows * members.shape[1] // experts_all
    expert_weights = (expert_gate, expert_up, expert_down)
    shared_weights = (shared_gate, shared_up, shared_down)

    rows_c, rows_b = tok_rows // 2, tok_rows * 3 // 8
    c = tokens[None, :rows_c]
    b = tokens[None, rows_c : rows_c + rows_b]
    a = tokens[None, rows_c + rows_b :]
    table = route_table(group_choice, members, route_weight, expert_home, capacity)

    c1, c3, cx0, ax, by = (
        send(c, Z_UP),
        send(c, Z_DOWN),
        send(c, ALONG_X),
        send(a, ALONG_X),
        send(b, ALONG_Y),
    )
    received = lax.all_to_all(table, AXES, split_axis=0, concat_axis=0, tiled=True)
    c, b, a, c1, c3, cx0, ax, by = barrier(c, b, a, c1, c3, cx0, ax, by)
    c0, b0, a0 = join(c, cx0, axis=0), join(b, by, axis=0), join(a, ax, axis=0)
    c13 = jnp.stack([c1, c3])[:, 0]

    c2, b1, b3, cx13, bx0, cy0, ay = (
        send(c1, Z_UP),
        send(b0, Z_UP),
        send(b0, Z_DOWN),
        send(c13, ALONG_X),
        send(b0, ALONG_X),
        send(c0, ALONG_Y),
        send(a0, ALONG_Y),
    )
    c0, b0, a0, c13, c2, b1, b3, cx13, bx0, cy0, ay = barrier(
        c0, b0, a0, c13, c2, b1, b3, cx13, bx0, cy0, ay
    )
    a0 = join(a0, ay, axis=0)
    b13 = jnp.stack([b1, b3])
    c13 = jnp.stack([c13, cx13], axis=1)
    whole0 = jnp.stack(
        [
            jnp.concatenate([c0[0], b0[0], a0[0]]),
            jnp.concatenate([c0[1], bx0[0], a0[1]]),
            jnp.concatenate([cy0[0], b0[1], a0[2]]),
            jnp.concatenate([cy0[1], bx0[1], a0[3]]),
        ]
    )[None]

    b2, a1, a3, cx2, bx13, cy13, other0 = (
        send(b1, Z_UP),
        send(a0, Z_UP),
        send(a0, Z_DOWN),
        send(c2, ALONG_X),
        send(b13, ALONG_X),
        send(c13, ALONG_Y),
        send(whole0, CORE),
    )
    b13, c13, c2, whole0, b2, a1, a3, cx2, bx13, cy13, other0 = barrier(
        b13, c13, c2, whole0, b2, a1, a3, cx2, bx13, cy13, other0
    )
    c2 = join(c2, cx2, axis=0)
    a13 = jnp.stack([a1, a3])
    whole13 = jnp.stack(
        [
            jnp.concatenate([c13[:, 0], b13[:, 0], a13[:, 0]], axis=1),
            jnp.concatenate([c13[:, 1], bx13[:, 0], a13[:, 1]], axis=1),
            jnp.concatenate([cy13[:, 0], b13[:, 1], a13[:, 2]], axis=1),
            jnp.concatenate([cy13[:, 1], bx13[:, 1], a13[:, 3]], axis=1),
        ],
        axis=1,
    )

    a2, bx2, cy2, other13 = (
        send(a1, Z_UP),
        send(b2, ALONG_X),
        send(c2, ALONG_Y),
        send(whole13, CORE),
    )
    whole2 = jnp.stack(
        [
            jnp.concatenate([c2[0], b2[0], a2[0]]),
            jnp.concatenate([c2[1], bx2[0], a2[1]]),
            jnp.concatenate([cy2[0], b2[1], a2[2]]),
            jnp.concatenate([cy2[1], bx2[1], a2[3]]),
        ]
    )[None]
    other2 = send(whole2, CORE)

    node, local = lax.axis_index("node"), lax.axis_index("local")
    z, y, x, core = node // 2, node % 2, local // 2, local % 2
    order = []
    for far_z in range(Z_COUNT):
        for far_core in range(2):
            for far_y in range(2):
                for far_x in range(2):
                    source = ((z - far_z) % Z_COUNT * 2 + (y ^ far_y)) * 2 + (x ^ far_x)
                    order.append(source * 2 + (core ^ far_core))
    weights = jnp.take(received, jnp.stack(order), axis=0)
    weights13 = join(weights[8:16], weights[24:32], axis=0)

    own0, far0 = expert_chunk(weights[:8], whole0, other0, expert_weights, shared_weights, capacity)
    own13, far13 = expert_chunk(weights13, whole13, other13, expert_weights, (), capacity)
    own2, far2 = expert_chunk(weights[16:24], whole2, other2, expert_weights, (), capacity)

    def split(own, far):
        total = own.astype(F32) + send(far, CORE).astype(F32)
        part_c = total[:, :, :rows_c]
        part_b = total[:, :, rows_c : rows_c + rows_b]
        part_a = total[:, :, rows_c + rows_b :]
        return part_c, part_b, part_a

    def back(value, pairs):
        return send(value.astype(BF16), pairs).astype(F32)

    c2, b2, a2 = split(own2, far2)
    sa2 = back(a2[0], Z_DOWN)
    sb2 = back(b2[0, 1::2], ALONG_X)
    sc2 = back(c2[0, 2:], ALONG_Y)
    c13, b13, a13 = split(own13, far13)
    c2, b2 = c2[0, :2], b2[0, 0::2]
    c2, b2, c13, b13, a13, sa2, sb2, sc2 = barrier(c2, b2, c13, b13, a13, sa2, sb2, sc2)
    c2, b2 = c2 + sc2, b2 + sb2
    a1, a3 = a13[0] + sa2, a13[1]
    sb = back(b2, Z_DOWN)
    sa1 = back(a1, Z_DOWN)
    sa3 = back(a3, Z_UP)
    sc2 = back(c2[1], ALONG_X)
    sb13 = back(b13[:, 1::2], ALONG_X)
    sc13 = back(c13[:, 2:], ALONG_Y)
    c0, b0, a0 = split(own0, far0)
    c2, b13, c13 = c2[0], b13[:, 0::2], c13[:, :2]
    c2, b13, c13, c0, b0, a0, sb, sa1, sa3, sc2, sb13, sc13 = barrier(
        c2, b13, c13, c0, b0, a0, sb, sa1, sa3, sc2, sb13, sc13
    )
    c2 = c2 + sc2
    b1, b3 = b13[0] + sb13[0] + sb, b13[1] + sb13[1]
    c13 = c13 + sc13
    a0 = a0[0] + sa1 + sa3
    sc = back(c2, Z_DOWN)
    sb1 = back(b1, Z_DOWN)
    sb3 = back(b3, Z_UP)
    sc13 = back(c13[:, 1], ALONG_X)
    sb0 = back(b0[0, 1::2], ALONG_X)
    sc0 = back(c0[0, 2:], ALONG_Y)
    sa0 = back(a0[2:], ALONG_Y)
    c13, b0, c0, a0 = c13[:, 0], b0[0, 0::2], c0[0, :2], a0[:2]
    c13, b0, c0, a0, sc, sb1, sb3, sc13, sb0, sc0, sa0 = barrier(
        c13, b0, c0, a0, sc, sb1, sb3, sc13, sb0, sc0, sa0
    )
    c1, c3 = c13[0] + sc13[0] + sc, c13[1] + sc13[1]
    b0 = b0 + sb0 + sb1 + sb3
    c0 = c0 + sc0
    a0 = a0 + sa0
    sc1 = back(c1, Z_DOWN)
    sc3 = back(c3, Z_UP)
    sc0 = back(c0[1], ALONG_X)
    sa0 = back(a0[1], ALONG_X)
    sb0 = back(b0[1], ALONG_Y)
    return jnp.concatenate([c0[0] + sc0 + sc1 + sc3, b0[0] + sb0, a0[0] + sa0]).astype(BF16)


def exchange_device(
    tokens,
    group_choice,
    members,
    route_weight,
    expert_home,
    expert_gate,
    expert_up,
    expert_down,
    shared_gate,
    shared_up,
    shared_down,
):
    node_count = lax.axis_size("node")
    local_count = lax.axis_size("local")
    device_count = node_count * local_count
    tok_rows, model_width = tokens.shape
    top_count = members.shape[1]
    experts_all = expert_home.shape[0]
    per_group = experts_all // GROUPS
    capacity = 2 * tok_rows * top_count // experts_all
    chosen = jnp.repeat(group_choice, 2, axis=1) * per_group + members
    onehot = (chosen[:, :, None] == jnp.arange(experts_all, dtype=jnp.int32)[None, None, :]).astype(
        jnp.int32
    )
    target = jnp.sum(onehot * expert_home[None, None, :], axis=-1)
    flat_hits = onehot.reshape(tok_rows * top_count, experts_all)
    before = jnp.cumsum(flat_hits, axis=0) - flat_hits
    position = jnp.sum(before * flat_hits, axis=-1).reshape(tok_rows, top_count)
    keep_mask = position < capacity
    slot_index = jnp.where(keep_mask, target * capacity + position, device_count * capacity)
    token_id = jnp.broadcast_to(
        jnp.arange(tok_rows, dtype=jnp.int32)[:, None], (tok_rows, top_count)
    )
    source_row = (
        jnp.full((device_count * capacity,), tok_rows, jnp.int32)
        .at[slot_index.reshape(-1)]
        .set(token_id.reshape(-1), mode="drop")
    )
    padded = jnp.concatenate([tokens, jnp.zeros((1, model_width), tokens.dtype)], axis=0)
    outgoing = padded[source_row].reshape(device_count, capacity, model_width)
    local_gate = expert_gate[0]
    local_up = expert_up[0]
    local_down = expert_down[0]
    arrived = lax.all_to_all(outgoing, ("node", "local"), split_axis=0, concat_axis=0, tiled=True)
    block_shape = arrived.shape
    row_block = arrived.reshape(-1, model_width)
    gate_part = jnp.dot(row_block, local_gate, preferred_element_type=jnp.float32)
    up_part = jnp.dot(row_block, local_up, preferred_element_type=jnp.float32)
    hidden = (jax.nn.silu(gate_part) * up_part).astype(jnp.bfloat16)
    result = jnp.dot(hidden, local_down, preferred_element_type=jnp.float32).astype(jnp.bfloat16)
    answered = lax.all_to_all(
        result.reshape(block_shape), ("node", "local"), split_axis=0, concat_axis=0, tiled=True
    )
    answered = answered.reshape(device_count * capacity, model_width)
    picked = answered[jnp.minimum(slot_index, device_count * capacity - 1)]
    weight = jnp.where(keep_mask, route_weight, 0.0)
    routed = jnp.zeros((tok_rows, model_width), jnp.float32)
    for choice_index in range(top_count):
        routed = routed + weight[:, choice_index, None] * picked[:, choice_index].astype(
            jnp.float32
        )
    node_rows = lax.all_gather(tokens, "local", axis=0, tiled=True)
    shared_hidden = (
        jax.nn.silu(jnp.dot(node_rows, shared_gate, preferred_element_type=jnp.float32))
        * jnp.dot(node_rows, shared_up, preferred_element_type=jnp.float32)
    ).astype(jnp.bfloat16)
    shared_part = lax.psum_scatter(
        jnp.dot(shared_hidden, shared_down, preferred_element_type=jnp.float32),
        "local",
        scatter_dimension=0,
        tiled=True,
    )
    return (routed + shared_part).astype(jnp.bfloat16)


def solution(mesh):
    in_specs = (
        P(("node", "local"), None),
        P(("node", "local"), None),
        P(("node", "local"), None),
        P(("node", "local"), None),
        P(),
        P(("node", "local"), None, None),
        P(("node", "local"), None, None),
        P(("node", "local"), None, None),
        P(None, "local"),
        P(None, "local"),
        P("local", None),
    )
    out_specs = P(("node", "local"), None)
    whole_gather = mesh.shape["node"] == 2 * Z_COUNT and mesh.shape["local"] == 4
    return jax.shard_map(
        block_device if whole_gather else exchange_device,
        mesh=mesh,
        in_specs=in_specs,
        out_specs=out_specs,
        check_vma=False,
    )
```

```python
import functools

import jax
import jax.numpy as jnp
from jax import lax
from jax.experimental import pallas as pl
from jax.experimental.pallas import tpu as pltpu
from jax.sharding import PartitionSpec as P

GROUPS = 8
AXES = ("node", "local")
F32 = jnp.float32
BF16 = jnp.bfloat16

Z_COUNT = 4


def permutation(move):
    pairs = []
    for z in range(Z_COUNT):
        for y in range(2):
            for x in range(2):
                for core in range(2):
                    to_z, to_y, to_x, to_core = move(z, y, x, core)
                    pairs.append(
                        (
                            ((z * 2 + y) * 2 + x) * 2 + core,
                            (((to_z % Z_COUNT) * 2 + to_y) * 2 + to_x) * 2 + to_core,
                        )
                    )
    return pairs


CORE = permutation(lambda z, y, x, core: (z, y, x, 1 - core))
ALONG_X = permutation(lambda z, y, x, core: (z, y, 1 - x, core))
ALONG_Y = permutation(lambda z, y, x, core: (z, 1 - y, x, core))
Z_UP = permutation(lambda z, y, x, core: (z + 1, y, x, core))
Z_DOWN = permutation(lambda z, y, x, core: (z - 1, y, x, core))


def send(value, pairs):
    return lax.ppermute(value, AXES, pairs)


def join(*values, axis=1):
    return jnp.concatenate(values, axis=axis)


def barrier(*values):
    return lax.optimization_barrier(values)


def expert_kernel(
    chunks, shared, capacity, weight_ref, token_hbm, gate_hbm, up_hbm, down_hbm, *rest
):
    if shared:
        sgate_hbm, sup_hbm, sdown_hbm = rest[:3]
        rest = rest[3:]
    out_hbm, held, gate, up, down, rows, hidden, answers, totals = rest[:9]
    rest = rest[9:]
    if shared:
        sgate, sup, sdown, shidden = rest[:4]
        rest = rest[4:]
    token_sem, gate_sem, up_sem, down_sem, out_sem = rest[:5]
    source_count = len(chunks) * 4
    tokens, width = held.shape[1:]
    inner = gate.shape[1]
    tile, out_tile = UP_TILE, DOWN_TILE

    copies = []
    for index in range(source_count):
        copies.append(
            pltpu.make_async_copy(
                token_hbm.at[chunks[index // 4], index % 4], held.at[index], token_sem.at[index]
            )
        )
    up_copies, down_copies = [], []
    for step in range(inner // tile):
        columns = pl.ds(step * tile, tile)
        up_copies.append(
            (
                pltpu.make_async_copy(gate_hbm.at[0, :, columns], gate.at[:, columns], gate_sem.at[step]),
                pltpu.make_async_copy(up_hbm.at[0, :, columns], up.at[:, columns], up_sem.at[step]),
            )
        )
    for step in range(width // out_tile):
        columns = pl.ds(step * out_tile, out_tile)
        down_copies.append(
            pltpu.make_async_copy(down_hbm.at[0, :, columns], down.at[:, columns], down_sem.at[step])
        )
    shared_copies = []
    if shared:
        shared_sem = rest[5]
        for number, (source, target) in enumerate(
            ((sgate_hbm, sgate), (sup_hbm, sup), (sdown_hbm, sdown))
        ):
            shared_copies.append(pltpu.make_async_copy(source, target, shared_sem.at[number]))
    for copy in copies:
        copy.start()
    for pair in up_copies:
        pair[0].start()
        pair[1].start()
    for copy in shared_copies + down_copies:
        copy.start()

    weights = weight_ref[...]
    hits = (weights > 0.0).astype(BF16)
    earlier = (
        lax.broadcasted_iota(jnp.int32, (tokens, tokens), 0)
        < lax.broadcasted_iota(jnp.int32, (tokens, tokens), 1)
    ).astype(BF16)
    place = jnp.dot(hits, earlier, preferred_element_type=F32).astype(jnp.int32)
    slots = lax.broadcasted_iota(jnp.int32, (capacity, tokens), 0)
    for index in range(source_count):
        chosen = (place[index : index + 1] == slots) & (weights[index : index + 1] > 0.0)
        copies[index].wait()
        rows[pl.ds(index * capacity, capacity)] = jnp.dot(
            chosen.astype(BF16), held[index], preferred_element_type=F32
        ).astype(BF16)

    for step in range(inner // tile):
        columns = pl.ds(step * tile, tile)
        up_copies[step][0].wait()
        up_copies[step][1].wait()
        gate_part = jnp.dot(rows[...], gate[:, columns], preferred_element_type=F32)
        up_part = jnp.dot(rows[...], up[:, columns], preferred_element_type=F32)
        hidden[:, columns] = (gate_part / (1.0 + jnp.exp(-gate_part)) * up_part).astype(BF16)

    if shared:
        shared_copies[0].wait()
        shared_copies[1].wait()
        shared_copies[2].wait()
        shared_rows = jnp.concatenate([held[0], held[1]], axis=0)
        gate_part = jnp.dot(shared_rows, sgate[...], preferred_element_type=F32)
        up_part = jnp.dot(shared_rows, sup[...], preferred_element_type=F32)
        shidden[...] = (gate_part / (1.0 + jnp.exp(-gate_part)) * up_part).astype(BF16)

    out_copies = []
    for step in range(width // out_tile):
        columns = pl.ds(step * out_tile, out_tile)
        down_copies[step].wait()
        answers[...] = jnp.dot(
            hidden[...], down[:, columns], preferred_element_type=F32
        ).astype(BF16)
        for index in range(source_count):
            weight_row = weights[index : index + 1]
            chosen = (place[index : index + 1] == slots) & (weight_row > 0.0)
            spread = jnp.where(chosen, jnp.broadcast_to(weight_row, chosen.shape), 0.0)
            high = spread.astype(BF16)
            low = (spread - high.astype(F32)).astype(BF16)
            answer = answers[pl.ds(index * capacity, capacity)]
            total = lax.dot_general(
                jnp.concatenate([high, low], axis=0),
                jnp.concatenate([answer, answer], axis=0),
                (((0,), (0,)), ((), ())),
                preferred_element_type=F32,
            )
            if shared and index < 2:
                total = total + jnp.dot(
                    shidden[pl.ds(index * tokens, tokens)],
                    sdown[:, columns],
                    preferred_element_type=F32,
                )
            totals[index, :, columns] = total.astype(BF16)
        out_copies.append(
            pltpu.make_async_copy(totals.at[:, :, columns], out_hbm.at[:, :, columns], out_sem.at[step])
        )
        out_copies[-1].start()
    for copy in out_copies:
        copy.wait()


UP_TILE = 256
DOWN_TILE = 512


def expert_half(weights, token_blocks, chunks, expert_weights, shared_weights, capacity):
    tokens, width = token_blocks.shape[2:]
    source_count = len(chunks) * 4
    inner = expert_weights[0].shape[2]
    up_steps, down_steps = inner // UP_TILE, width // DOWN_TILE
    scratch = [
        pltpu.VMEM((source_count, tokens, width), BF16),
        pltpu.VMEM((width, inner), BF16),
        pltpu.VMEM((width, inner), BF16),
        pltpu.VMEM((inner, width), BF16),
        pltpu.VMEM((source_count * capacity, width), BF16),
        pltpu.VMEM((source_count * capacity, inner), BF16),
        pltpu.VMEM((source_count * capacity, DOWN_TILE), BF16),
        pltpu.VMEM((source_count, tokens, width), BF16),
    ]
    if shared_weights:
        shared_width = shared_weights[0].shape[1]
        scratch += [
            pltpu.VMEM((width, shared_width), BF16),
            pltpu.VMEM((width, shared_width), BF16),
            pltpu.VMEM((shared_width, width), BF16),
            pltpu.VMEM((2 * tokens, shared_width), BF16),
        ]
    scratch += [pltpu.SemaphoreType.DMA((count,)) for count in (source_count, up_steps, up_steps, down_steps, down_steps)]
    if shared_weights:
        scratch.append(pltpu.SemaphoreType.DMA((3,)))
    flops = 2 * source_count * capacity * (3 * width * inner + 2 * tokens * width)
    operands = (weights, token_blocks, *expert_weights, *shared_weights)
    out = pl.pallas_call(
        functools.partial(expert_kernel, chunks, len(shared_weights) > 0, capacity),
        out_shape=jax.ShapeDtypeStruct((source_count, tokens, width), BF16),
        in_specs=[pl.BlockSpec(memory_space=pltpu.VMEM)]
        + [pl.BlockSpec(memory_space=pl.ANY)] * (len(operands) - 1),
        out_specs=pl.BlockSpec(memory_space=pl.ANY),
        scratch_shapes=scratch,
        cost_estimate=pl.CostEstimate(
            flops=flops,
            bytes_accessed=3 * width * inner * 2 + 4 * source_count * tokens * width,
            transcendentals=0,
        ),
        compiler_params=pltpu.CompilerParams(vmem_limit_bytes=VMEM_LIMIT),
    )(*operands)
    return out.reshape(len(chunks), 4, tokens, width)


VMEM_LIMIT = 32 * 1024 * 1024


def route_table(group_choice, members, route_weight, expert_home, capacity):
    tok_rows = members.shape[0]
    experts_all = expert_home.shape[0]
    per_group = experts_all // GROUPS
    chosen = jnp.repeat(group_choice, 2, axis=1) * per_group + members
    ids = jnp.arange(experts_all, dtype=jnp.int32)
    target = jnp.sum(
        jnp.where(chosen[:, :, None] == ids[None, None, :], expert_home[None, None, :], 0), axis=-1
    )
    table = jnp.sum(
        jnp.where(target[:, :, None] == ids[None, None, :], route_weight[:, :, None], 0.0), axis=1
    )
    hits = (table > 0.0).astype(BF16)
    earlier = (
        lax.broadcasted_iota(jnp.int32, (tok_rows, tok_rows), 0)
        > lax.broadcasted_iota(jnp.int32, (tok_rows, tok_rows), 1)
    ).astype(BF16)
    place = jnp.dot(earlier, hits, preferred_element_type=F32)
    table = jnp.where(place < capacity, table, 0.0)
    return table.T


def block_device(
    tokens,
    group_choice,
    members,
    route_weight,
    expert_home,
    expert_gate,
    expert_up,
    expert_down,
    shared_gate,
    shared_up,
    shared_down,
):
    tok_rows, width = tokens.shape
    experts_all = expert_home.shape[0]
    capacity = 2 * tok_rows * members.shape[1] // experts_all
    expert_weights = (expert_gate, expert_up, expert_down)
    shared_weights = (shared_gate, shared_up, shared_down)

    rows_c, rows_b = tok_rows // 2, tok_rows * 3 // 8
    c = tokens[None, :rows_c]
    b = tokens[None, rows_c : rows_c + rows_b]
    a = tokens[None, rows_c + rows_b :]
    table = route_table(group_choice, members, route_weight, expert_home, capacity)

    c1, c3, cx0, ax, by = (
        send(c, Z_UP),
        send(c, Z_DOWN),
        send(c, ALONG_X),
        send(a, ALONG_X),
        send(b, ALONG_Y),
    )
    c, b, a, c1, c3, cx0, ax, by, table = barrier(c, b, a, c1, c3, cx0, ax, by, table)
    c0, b0, a0 = join(c, cx0, axis=0), join(b, by, axis=0), join(a, ax, axis=0)
    c13 = jnp.stack([c1, c3])[:, 0]

    c2, b1, b3, cx13, bx0, cy0, ay = (
        send(c1, Z_UP),
        send(b0, Z_UP),
        send(b0, Z_DOWN),
        send(c13, ALONG_X),
        send(b0, ALONG_X),
        send(c0, ALONG_Y),
        send(a0, ALONG_Y),
    )
    received = lax.all_to_all(table, AXES, split_axis=0, concat_axis=0, tiled=True)
    c0, b0, a0, c13, c2, b1, b3, cx13, bx0, cy0, ay, received = barrier(
        c0, b0, a0, c13, c2, b1, b3, cx13, bx0, cy0, ay, received
    )
    a0 = join(a0, ay, axis=0)
    b13 = jnp.stack([b1, b3])
    c13 = jnp.stack([c13, cx13], axis=1)
    whole0 = jnp.stack(
        [
            jnp.concatenate([c0[0], b0[0], a0[0]]),
            jnp.concatenate([c0[1], bx0[0], a0[1]]),
            jnp.concatenate([cy0[0], b0[1], a0[2]]),
            jnp.concatenate([cy0[1], bx0[1], a0[3]]),
        ]
    )[None]


    node, local = lax.axis_index("node"), lax.axis_index("local")
    z, y, x, core = node // 2, node % 2, local // 2, local % 2
    order = []
    for far_z in range(Z_COUNT):
        for far_core in range(2):
            for far_y in range(2):
                for far_x in range(2):
                    source = ((z - far_z) % Z_COUNT * 2 + (y ^ far_y)) * 2 + (x ^ far_x)
                    order.append(source * 2 + (core ^ far_core))
    weights = jnp.take(received, jnp.stack(order), axis=0)

    def expert(k, core, token_blocks, chunks=(0,)):
        rows = weights[k * 8 + core * 4 : k * 8 + core * 4 + 4]
        if len(chunks) == 2:
            rows = join(rows, weights[24 + core * 4 : 28 + core * 4], axis=0)
        shared = shared_weights if k == 0 else ()
        return expert_half(rows, token_blocks, chunks, expert_weights, shared, capacity)

    b2, a1, a3, cx2, bx13, cy13, other0 = (
        send(b1, Z_UP),
        send(a0, Z_UP),
        send(a0, Z_DOWN),
        send(c2, ALONG_X),
        send(b13, ALONG_X),
        send(c13, ALONG_Y),
        send(whole0, CORE),
    )
    own0 = expert(0, 0, whole0)
    b13, c13, c2, b2, a1, a3, cx2, bx13, cy13, other0, own0 = barrier(
        b13, c13, c2, b2, a1, a3, cx2, bx13, cy13, other0, own0
    )
    c2 = join(c2, cx2, axis=0)
    a13 = jnp.stack([a1, a3])
    whole13 = jnp.stack(
        [
            jnp.concatenate([c13[:, 0], b13[:, 0], a13[:, 0]], axis=1),
            jnp.concatenate([c13[:, 1], bx13[:, 0], a13[:, 1]], axis=1),
            jnp.concatenate([cy13[:, 0], b13[:, 1], a13[:, 2]], axis=1),
            jnp.concatenate([cy13[:, 1], bx13[:, 1], a13[:, 3]], axis=1),
        ],
        axis=1,
    )

    a2, bx2, cy2, other13 = (
        send(a1, Z_UP),
        send(b2, ALONG_X),
        send(c2, ALONG_Y),
        send(whole13, CORE),
    )
    far0 = expert(0, 1, other0)
    own13 = expert(1, 0, whole13, (0, 1))
    c2, b2, a2, bx2, cy2, other13, far0, own13 = barrier(
        c2, b2, a2, bx2, cy2, other13, far0, own13
    )
    whole2 = jnp.stack(
        [
            jnp.concatenate([c2[0], b2[0], a2[0]]),
            jnp.concatenate([c2[1], bx2[0], a2[1]]),
            jnp.concatenate([cy2[0], b2[1], a2[2]]),
            jnp.concatenate([cy2[1], bx2[1], a2[3]]),
        ]
    )[None]

    other2 = send(whole2, CORE)
    own2 = expert(2, 0, whole2)
    back0 = send(far0, CORE)
    other2, own2, back0 = barrier(other2, own2, back0)
    far2 = expert(2, 1, other2)


    def split(own, other):
        def total(blocks, tokens):
            return own[:, blocks, tokens].astype(F32) + other[:, blocks, tokens].astype(F32)

        only_c, only_b = slice(0, rows_c), slice(rows_c, rows_c + rows_b)
        return (
            total(slice(0, 2), only_c),
            total(slice(2, 4), only_c).astype(BF16),
            total(slice(0, 4, 2), only_b),
            total(slice(1, 4, 2), only_b).astype(BF16),
            total(slice(0, 4), slice(rows_c + rows_b, None)),
        )

    def back(value, pairs):
        return send(value.astype(BF16), pairs).astype(F32)

    back2 = send(far2, CORE)
    far1 = expert(1, 1, other13, (0,))
    back2, far1 = barrier(back2, far1)
    c2, c2_far, b2, b2_far, a2 = split(own2, back2)
    sa2 = back(a2[0], Z_DOWN)
    sb2 = back(b2_far[0], ALONG_X)
    sc2 = back(c2_far[0], ALONG_Y)
    back1 = send(far1, CORE)
    far3 = expert(3, 1, other13, (1,))
    back3 = send(far3, CORE)
    c2, b2, back1, back3, sa2, sb2, sc2 = barrier(c2, b2, back1, back3, sa2, sb2, sc2)
    c2, b2 = c2[0] + sc2, b2[0] + sb2
    c13, c13_far, b13, b13_far, a13 = split(own13, join(back1, back3, axis=0))
    a1, a3 = a13[0] + sa2, a13[1]
    sb = back(b2, Z_DOWN)
    sa1 = back(a1, Z_DOWN)
    sa3 = back(a3, Z_UP)
    sc2 = back(c2[1], ALONG_X)
    sb13 = back(b13_far, ALONG_X)
    sc13 = back(c13_far, ALONG_Y)
    c2 = c2[0]
    c2, b13, c13, sb, sa1, sa3, sc2, sb13, sc13 = barrier(
        c2, b13, c13, sb, sa1, sa3, sc2, sb13, sc13
    )
    c0, c0_far, b0, b0_far, a0 = split(own0, back0)
    c2 = c2 + sc2
    b1, b3 = b13[0] + sb13[0] + sb, b13[1] + sb13[1]
    c13 = c13 + sc13
    a0 = a0[0] + sa1 + sa3
    sc = back(c2, Z_DOWN)
    sb1 = back(b1, Z_DOWN)
    sb3 = back(b3, Z_UP)
    sc13 = back(c13[:, 1], ALONG_X)
    sb0 = back(b0_far[0], ALONG_X)
    sc0 = back(c0_far[0], ALONG_Y)
    sa0 = back(a0[2:], ALONG_Y)
    c13, b0, c0, a0 = c13[:, 0], b0[0], c0[0], a0[:2]
    c13, b0, c0, a0, sc, sb1, sb3, sc13, sb0, sc0, sa0 = barrier(
        c13, b0, c0, a0, sc, sb1, sb3, sc13, sb0, sc0, sa0
    )
    c1, c3 = c13[0] + sc13[0] + sc, c13[1] + sc13[1]
    b0 = b0 + sb0 + sb1 + sb3
    c0 = c0 + sc0
    a0 = a0 + sa0
    sc1 = back(c1, Z_DOWN)
    sc3 = back(c3, Z_UP)
    sc0 = back(c0[1], ALONG_X)
    sa0 = back(a0[1], ALONG_X)
    sb0 = back(b0[1], ALONG_Y)
    return jnp.concatenate([c0[0] + sc0 + sc1 + sc3, b0[0] + sb0, a0[0] + sa0]).astype(BF16)


def exchange_device(
    tokens,
    group_choice,
    members,
    route_weight,
    expert_home,
    expert_gate,
    expert_up,
    expert_down,
    shared_gate,
    shared_up,
    shared_down,
):
    node_count = lax.axis_size("node")
    local_count = lax.axis_size("local")
    device_count = node_count * local_count
    tok_rows, model_width = tokens.shape
    top_count = members.shape[1]
    experts_all = expert_home.shape[0]
    per_group = experts_all // GROUPS
    capacity = 2 * tok_rows * top_count // experts_all
    chosen = jnp.repeat(group_choice, 2, axis=1) * per_group + members
    onehot = (chosen[:, :, None] == jnp.arange(experts_all, dtype=jnp.int32)[None, None, :]).astype(
        jnp.int32
    )
    target = jnp.sum(onehot * expert_home[None, None, :], axis=-1)
    flat_hits = onehot.reshape(tok_rows * top_count, experts_all)
    before = jnp.cumsum(flat_hits, axis=0) - flat_hits
    position = jnp.sum(before * flat_hits, axis=-1).reshape(tok_rows, top_count)
    keep_mask = position < capacity
    slot_index = jnp.where(keep_mask, target * capacity + position, device_count * capacity)
    token_id = jnp.broadcast_to(
        jnp.arange(tok_rows, dtype=jnp.int32)[:, None], (tok_rows, top_count)
    )
    source_row = (
        jnp.full((device_count * capacity,), tok_rows, jnp.int32)
        .at[slot_index.reshape(-1)]
        .set(token_id.reshape(-1), mode="drop")
    )
    padded = jnp.concatenate([tokens, jnp.zeros((1, model_width), tokens.dtype)], axis=0)
    outgoing = padded[source_row].reshape(device_count, capacity, model_width)
    local_gate = expert_gate[0]
    local_up = expert_up[0]
    local_down = expert_down[0]
    arrived = lax.all_to_all(outgoing, ("node", "local"), split_axis=0, concat_axis=0, tiled=True)
    block_shape = arrived.shape
    row_block = arrived.reshape(-1, model_width)
    gate_part = jnp.dot(row_block, local_gate, preferred_element_type=jnp.float32)
    up_part = jnp.dot(row_block, local_up, preferred_element_type=jnp.float32)
    hidden = (jax.nn.silu(gate_part) * up_part).astype(jnp.bfloat16)
    result = jnp.dot(hidden, local_down, preferred_element_type=jnp.float32).astype(jnp.bfloat16)
    answered = lax.all_to_all(
        result.reshape(block_shape), ("node", "local"), split_axis=0, concat_axis=0, tiled=True
    )
    answered = answered.reshape(device_count * capacity, model_width)
    picked = answered[jnp.minimum(slot_index, device_count * capacity - 1)]
    weight = jnp.where(keep_mask, route_weight, 0.0)
    routed = jnp.zeros((tok_rows, model_width), jnp.float32)
    for choice_index in range(top_count):
        routed = routed + weight[:, choice_index, None] * picked[:, choice_index].astype(
            jnp.float32
        )
    node_rows = lax.all_gather(tokens, "local", axis=0, tiled=True)
    shared_hidden = (
        jax.nn.silu(jnp.dot(node_rows, shared_gate, preferred_element_type=jnp.float32))
        * jnp.dot(node_rows, shared_up, preferred_element_type=jnp.float32)
    ).astype(jnp.bfloat16)
    shared_part = lax.psum_scatter(
        jnp.dot(shared_hidden, shared_down, preferred_element_type=jnp.float32),
        "local",
        scatter_dimension=0,
        tiled=True,
    )
    return (routed + shared_part).astype(jnp.bfloat16)


def solution(mesh):
    in_specs = (
        P(("node", "local"), None),
        P(("node", "local"), None),
        P(("node", "local"), None),
        P(("node", "local"), None),
        P(),
        P(("node", "local"), None, None),
        P(("node", "local"), None, None),
        P(("node", "local"), None, None),
        P(None, "local"),
        P(None, "local"),
        P("local", None),
    )
    out_specs = P(("node", "local"), None)
    whole_gather = mesh.shape["node"] == 2 * Z_COUNT and mesh.shape["local"] == 4
    return jax.shard_map(
        block_device if whole_gather else exchange_device,
        mesh=mesh,
        in_specs=in_specs,
        out_specs=out_specs,
        check_vma=False,
    )
```

```python
import functools

import jax
import jax.numpy as jnp
from jax import lax
from jax.experimental import pallas as pl
from jax.experimental.pallas import tpu as pltpu
from jax.sharding import PartitionSpec as P

GROUPS = 8
AXES = ("node", "local")
F32 = jnp.float32
BF16 = jnp.bfloat16

Z_COUNT = 4


def permutation(move):
    pairs = []
    for z in range(Z_COUNT):
        for y in range(2):
            for x in range(2):
                for core in range(2):
                    to_z, to_y, to_x, to_core = move(z, y, x, core)
                    pairs.append(
                        (
                            ((z * 2 + y) * 2 + x) * 2 + core,
                            (((to_z % Z_COUNT) * 2 + to_y) * 2 + to_x) * 2 + to_core,
                        )
                    )
    return pairs


CORE = permutation(lambda z, y, x, core: (z, y, x, 1 - core))
ALONG_X = permutation(lambda z, y, x, core: (z, y, 1 - x, core))
ALONG_Y = permutation(lambda z, y, x, core: (z, 1 - y, x, core))
Z_UP = permutation(lambda z, y, x, core: (z + 1, y, x, core))
Z_DOWN = permutation(lambda z, y, x, core: (z - 1, y, x, core))


def send(value, pairs):
    return lax.ppermute(value, AXES, pairs)


def join(*values):
    return jnp.concatenate(values, axis=0)


def barrier(*values):
    return lax.optimization_barrier(values)


def expert_kernel(
    base, shared, capacity, weight_ref, own_hbm, other_hbm, gate_hbm, up_hbm, down_hbm, *rest
):
    if shared:
        sgate_hbm, sup_hbm, sdown_hbm = rest[:3]
        rest = rest[3:]
    own_out, other_out, held, gate, up, down, rows, hidden, answers, totals = rest[:10]
    rest = rest[10:]
    if shared:
        sgate, sup, sdown, shidden = rest[:4]
        rest = rest[4:]
    token_sem, gate_sem, up_sem, down_sem, out_sem = rest[:5]
    source_count = 8
    tokens, width = held.shape[1:]
    inner = gate.shape[1]
    tile, out_tile = UP_TILE, DOWN_TILE

    copies = []
    for index in range(source_count):
        copies.append(
            pltpu.make_async_copy(
                (own_hbm, other_hbm)[index // 4].at[base + index % 4], held.at[index], token_sem.at[index]
            )
        )
    up_copies, down_copies = [], []
    for step in range(inner // tile):
        columns = pl.ds(step * tile, tile)
        up_copies.append(
            (
                pltpu.make_async_copy(gate_hbm.at[0, :, columns], gate.at[:, columns], gate_sem.at[step]),
                pltpu.make_async_copy(up_hbm.at[0, :, columns], up.at[:, columns], up_sem.at[step]),
            )
        )
    for step in range(width // out_tile):
        columns = pl.ds(step * out_tile, out_tile)
        down_copies.append(
            pltpu.make_async_copy(down_hbm.at[0, :, columns], down.at[:, columns], down_sem.at[step])
        )
    shared_copies = []
    if shared:
        shared_sem = rest[5]
        for number, (source, target) in enumerate(
            ((sgate_hbm, sgate), (sup_hbm, sup), (sdown_hbm, sdown))
        ):
            shared_copies.append(pltpu.make_async_copy(source, target, shared_sem.at[number]))
    waiting = [copy for pair in up_copies for copy in pair] + shared_copies + down_copies

    def start_more(count):
        for _ in range(min(count, len(waiting))):
            waiting.pop(0).start()

    for copy in copies:
        copy.start()
    start_more(2)

    weights = weight_ref[...]
    hits = (weights > 0.0).astype(BF16)
    earlier = (
        lax.broadcasted_iota(jnp.int32, (tokens, tokens), 0)
        < lax.broadcasted_iota(jnp.int32, (tokens, tokens), 1)
    ).astype(BF16)
    place = jnp.dot(hits, earlier, preferred_element_type=F32).astype(jnp.int32)
    slots = lax.broadcasted_iota(jnp.int32, (capacity, tokens), 0)
    for index in range(source_count):
        chosen = (place[index : index + 1] == slots) & (weights[index : index + 1] > 0.0)
        copies[index].wait()
        if index == source_count // 2:
            start_more(2)
        rows[pl.ds(index * capacity, capacity)] = jnp.dot(
            chosen.astype(BF16), held[index], preferred_element_type=F32
        ).astype(BF16)

    for step in range(inner // tile):
        columns = pl.ds(step * tile, tile)
        up_copies[step][0].wait()
        up_copies[step][1].wait()
        start_more(3)
        gate_part = jnp.dot(rows[...], gate[:, columns], preferred_element_type=F32)
        up_part = jnp.dot(rows[...], up[:, columns], preferred_element_type=F32)
        hidden[:, columns] = (gate_part / (1.0 + jnp.exp(-gate_part)) * up_part).astype(BF16)

    start_more(len(waiting))
    if shared:
        shared_copies[0].wait()
        shared_copies[1].wait()
        shared_copies[2].wait()
        shared_rows = jnp.concatenate([held[index] for index in SHARED_SOURCES], axis=0)
        gate_part = jnp.dot(shared_rows, sgate[...], preferred_element_type=F32)
        up_part = jnp.dot(shared_rows, sup[...], preferred_element_type=F32)
        shidden[...] = (gate_part / (1.0 + jnp.exp(-gate_part)) * up_part).astype(BF16)

    out_copies = []
    for step in range(width // out_tile):
        columns = pl.ds(step * out_tile, out_tile)
        down_copies[step].wait()
        answers[...] = jnp.dot(
            hidden[...], down[:, columns], preferred_element_type=F32
        ).astype(BF16)
        for index in range(source_count):
            weight_row = weights[index : index + 1]
            chosen = (place[index : index + 1] == slots) & (weight_row > 0.0)
            spread = jnp.where(chosen, jnp.broadcast_to(weight_row, chosen.shape), 0.0)
            high = spread.astype(BF16)
            low = (spread - high.astype(F32)).astype(BF16)
            answer = answers[pl.ds(index * capacity, capacity)]
            total = lax.dot_general(
                jnp.concatenate([high, low], axis=0),
                jnp.concatenate([answer, answer], axis=0),
                (((0,), (0,)), ((), ())),
                preferred_element_type=F32,
            )
            if shared and index in SHARED_SOURCES:
                total = total + jnp.dot(
                    shidden[pl.ds(SHARED_SOURCES.index(index) * tokens, tokens)],
                    sdown[:, columns],
                    preferred_element_type=F32,
                )
            totals[index, :, columns] = total.astype(BF16)
        for side, target in enumerate((own_out, other_out)):
            copy = pltpu.make_async_copy(
                totals.at[pl.ds(side * 4, 4), :, columns],
                target.at[:, :, columns],
                out_sem.at[step * 2 + side],
            )
            copy.start()
            out_copies.append(copy)
    for copy in out_copies:
        copy.wait()


UP_TILE = 256
DOWN_TILE = 512


SHARED_SOURCES = (0, 1, 4, 5)
VMEM_LIMIT = 44 * 1024 * 1024
FLOPS = 1000


def expert_chunk(weights, own, other, base, expert_weights, shared_weights, capacity):
    _, tokens, width = own.shape
    source_count = 8
    inner = expert_weights[0].shape[2]
    up_steps, down_steps = inner // UP_TILE, width // DOWN_TILE
    scratch = [
        pltpu.VMEM((source_count, tokens, width), BF16),
        pltpu.VMEM((width, inner), BF16),
        pltpu.VMEM((width, inner), BF16),
        pltpu.VMEM((inner, width), BF16),
        pltpu.VMEM((source_count * capacity, width), BF16),
        pltpu.VMEM((source_count * capacity, inner), BF16),
        pltpu.VMEM((source_count * capacity, DOWN_TILE), BF16),
        pltpu.VMEM((source_count, tokens, width), BF16),
    ]
    if shared_weights:
        shared_width = shared_weights[0].shape[1]
        scratch += [
            pltpu.VMEM((width, shared_width), BF16),
            pltpu.VMEM((width, shared_width), BF16),
            pltpu.VMEM((shared_width, width), BF16),
            pltpu.VMEM((len(SHARED_SOURCES) * tokens, shared_width), BF16),
        ]
    counts = (source_count, up_steps, up_steps, down_steps, 2 * down_steps)
    scratch += [pltpu.SemaphoreType.DMA((count,)) for count in counts]
    if shared_weights:
        scratch.append(pltpu.SemaphoreType.DMA((3,)))
    operands = (weights, own, other, *expert_weights, *shared_weights)
    return pl.pallas_call(
        functools.partial(expert_kernel, base, len(shared_weights) > 0, capacity),
        out_shape=[jax.ShapeDtypeStruct((4, tokens, width), BF16)] * 2,
        in_specs=[pl.BlockSpec(memory_space=pltpu.VMEM)]
        + [pl.BlockSpec(memory_space=pl.ANY)] * (len(operands) - 1),
        out_specs=[pl.BlockSpec(memory_space=pl.ANY)] * 2,
        scratch_shapes=scratch,
        cost_estimate=pl.CostEstimate(flops=FLOPS, bytes_accessed=FLOPS, transcendentals=0),
        compiler_params=pltpu.CompilerParams(vmem_limit_bytes=VMEM_LIMIT),
    )(*operands)


def route_table(group_choice, members, route_weight, expert_home, capacity):
    tok_rows = members.shape[0]
    experts_all = expert_home.shape[0]
    per_group = experts_all // GROUPS
    chosen = jnp.repeat(group_choice, 2, axis=1) * per_group + members
    ids = jnp.arange(experts_all, dtype=jnp.int32)
    target = jnp.sum(
        jnp.where(chosen[:, :, None] == ids[None, None, :], expert_home[None, None, :], 0), axis=-1
    )
    table = jnp.sum(
        jnp.where(target[:, :, None] == ids[None, None, :], route_weight[:, :, None], 0.0), axis=1
    )
    hits = (table > 0.0).astype(BF16)
    earlier = (
        lax.broadcasted_iota(jnp.int32, (tok_rows, tok_rows), 0)
        > lax.broadcasted_iota(jnp.int32, (tok_rows, tok_rows), 1)
    ).astype(BF16)
    place = jnp.dot(earlier, hits, preferred_element_type=F32)
    table = jnp.where(place < capacity, table, 0.0)
    return table.T


def block_device(
    tokens,
    group_choice,
    members,
    route_weight,
    expert_home,
    expert_gate,
    expert_up,
    expert_down,
    shared_gate,
    shared_up,
    shared_down,
):
    tok_rows, width = tokens.shape
    experts_all = expert_home.shape[0]
    capacity = 2 * tok_rows * members.shape[1] // experts_all
    expert_weights = (expert_gate, expert_up, expert_down)
    shared_weights = (shared_gate, shared_up, shared_down)

    rows_c, rows_b = tok_rows // 2, tok_rows * 3 // 8
    c = tokens[None, :rows_c]
    b = tokens[None, rows_c : rows_c + rows_b]
    a = tokens[None, rows_c + rows_b :]
    table = route_table(group_choice, members, route_weight, expert_home, capacity)

    c1, c3, cx0, ax, by = (
        send(c, Z_UP),
        send(c, Z_DOWN),
        send(c, ALONG_X),
        send(a, ALONG_X),
        send(b, ALONG_Y),
    )
    c, b, a, c1, c3, cx0, ax, by, table = barrier(c, b, a, c1, c3, cx0, ax, by, table)

    b0, c0, a0 = join(b, by), join(c, cx0), join(a, ax)
    c13 = jnp.stack([c1, c3])[:, 0]
    b1, b3, cy0, bx0, cx13, c2, ay = (
        send(b0, Z_UP),
        send(b0, Z_DOWN),
        send(c0, ALONG_Y),
        send(b0, ALONG_X),
        send(c13, ALONG_X),
        send(c1, Z_UP),
        send(a0, ALONG_Y),
    )
    received = lax.all_to_all(table, AXES, split_axis=0, concat_axis=0, tiled=True)
    c0, b0, a0, c13, c2, b1, b3, cx13, bx0, cy0, ay, received = barrier(
        c0, b0, a0, c13, c2, b1, b3, cx13, bx0, cy0, ay, received
    )

    node, local = lax.axis_index("node"), lax.axis_index("local")
    z, y, x, core = node // 2, node % 2, local // 2, local % 2
    order = []
    for far_z in range(Z_COUNT):
        for far_core in range(2):
            for far_y in range(2):
                for far_x in range(2):
                    source = ((z - far_z) % Z_COUNT * 2 + (y ^ far_y)) * 2 + (x ^ far_x)
                    order.append(source * 2 + (core ^ far_core))
    weights = jnp.take(received, jnp.stack(order), axis=0)

    def expert(k, own, other, base=0):
        shared = shared_weights if k == 0 else ()
        return expert_chunk(
            weights[k * 8 : k * 8 + 8], own, other, base, expert_weights, shared, capacity
        )

    def whole(c_near, c_far, b_near, b_far, part_a):
        return jnp.stack(
            [
                jnp.concatenate([c_near[0], b_near[0], part_a[0]]),
                jnp.concatenate([c_near[1], b_far[0], part_a[1]]),
                jnp.concatenate([c_far[0], b_near[1], part_a[2]]),
                jnp.concatenate([c_far[1], b_far[1], part_a[3]]),
            ]
        )

    a0 = join(a0, ay)
    b13 = jnp.stack([b1, b3])
    c13 = jnp.stack([c13, cx13], axis=1)
    whole0 = whole(c0, cy0, b0, bx0, a0)
    other0, cy13, bx13, b2, a1, cx2, a3 = (
        send(whole0, CORE),
        send(c13, ALONG_Y),
        send(b13, ALONG_X),
        send(b1, Z_UP),
        send(a0, Z_UP),
        send(c2, ALONG_X),
        send(a0, Z_DOWN),
    )
    own0, far0 = expert(0, whole0, other0)
    c13, b13, c2, b2, a1, a3, cx2, bx13, cy13, own0, far0 = barrier(
        c13, b13, c2, b2, a1, a3, cx2, bx13, cy13, own0, far0
    )

    rows_yx = tok_rows * 5 // 8
    only_c, only_b = slice(0, rows_yx), slice(rows_yx, None)
    near_y, far_y, near_x, far_x = slice(0, 2), slice(2, 4), slice(0, 4, 2), slice(1, 4, 2)

    def total(pair, blocks, part):
        return pair[0][blocks, part].astype(F32) + pair[1][blocks, part].astype(F32)

    def back(value, pairs):
        return send(value.astype(BF16), pairs)

    c2 = join(c2, cx2)
    a13 = jnp.stack([a1, a3])
    whole13 = jnp.stack(
        [
            jnp.concatenate([c13[:, 0], b13[:, 0], a13[:, 0]], axis=1),
            jnp.concatenate([c13[:, 1], bx13[:, 0], a13[:, 1]], axis=1),
            jnp.concatenate([cy13[:, 0], b13[:, 1], a13[:, 2]], axis=1),
            jnp.concatenate([cy13[:, 1], bx13[:, 1], a13[:, 3]], axis=1),
        ],
        axis=1,
    ).reshape(8, tok_rows, width)
    back0, cy2, bx2, a2, other13 = (
        send(far0, CORE),
        send(c2, ALONG_Y),
        send(b2, ALONG_X),
        send(a1, Z_UP),
        send(whole13, CORE),
    )
    pair0 = (own0, back0)
    sc0 = back(total(pair0, far_y, only_c), ALONG_Y)
    sb0 = back(total(pair0, far_x, only_b), ALONG_X)
    own1, far1 = expert(1, whole13, other13)
    c2, b2, a2, bx2, cy2, other13, whole13, own1, far1, sc0, sb0 = barrier(
        c2, b2, a2, bx2, cy2, other13, whole13, own1, far1, sc0, sb0
    )

    whole2 = whole(c2, cy2, b2, bx2, a2)
    other2, back1 = send(whole2, CORE), send(far1, CORE)
    pair1 = (own1, back1)
    sc1 = total(pair1, far_y, only_c).astype(BF16)
    sb1 = total(pair1, far_x, only_b).astype(BF16)
    sc1, sb1, whole2, other2 = barrier(sc1, sb1, whole2, other2)
    sc1, sb1 = send(sc1, ALONG_Y), send(sb1, ALONG_X)
    own2, far2 = expert(2, whole2, other2)
    sc1, sb1, own2, far2 = barrier(sc1, sb1, own2, far2)
    back2 = send(far2, CORE)
    pair2 = (own2, back2)
    sc2 = total(pair2, far_y, only_c).astype(BF16)
    sb2 = total(pair2, far_x, only_b).astype(BF16)
    c1 = total(pair1, near_y, only_c) + sc1
    tc1 = c1[1].astype(BF16)
    sc2, sb2, tc1, whole13, other13 = barrier(sc2, sb2, tc1, whole13, other13)

    sc2, sb2, tc1 = send(sc2, ALONG_Y), send(sb2, ALONG_X), send(tc1, ALONG_X)
    own3, far3 = expert(3, whole13, other13, 4)
    own3, far3, sb2, sc2, tc1 = barrier(own3, far3, sb2, sc2, tc1)

    back3 = send(far3, CORE)
    c2 = total(pair2, near_y, only_c) + sc2
    b2 = total(pair2, near_x, only_b) + sb2
    pair3 = (own3, back3)
    sb, tc2, sc3, sb3 = (
        back(b2, Z_DOWN),
        back(c2[1], ALONG_X),
        back(total(pair3, far_y, only_c), ALONG_Y),
        back(total(pair3, far_x, only_b), ALONG_X),
    )
    sb, tc2, sb3, sc3 = barrier(sb, tc2, sb3, sc3)

    c2 = c2[0] + tc2
    b1 = total(pair1, near_x, only_b) + sb1 + sb
    b3 = total(pair3, near_x, only_b) + sb3
    c3 = total(pair3, near_y, only_c) + sc3
    c0 = total(pair0, near_y, only_c) + sc0
    tb1, tb3, uc2, tc3, tc0 = (
        back(b1, Z_DOWN),
        back(b3, Z_UP),
        back(c2, Z_DOWN),
        back(c3[1], ALONG_X),
        back(c0[1], ALONG_X),
    )
    uc2, tb1, tb3, tc3, tc0 = barrier(uc2, tb1, tb3, tc3, tc0)

    c1 = c1[0] + tc1 + uc2
    c3 = c3[0] + tc3
    b0 = total(pair0, near_x, only_b) + sb0 + tb1 + tb3
    uc1, uc3, tb0 = back(c1, Z_DOWN), back(c3, Z_UP), back(b0[1], ALONG_Y)
    return jnp.concatenate([c0[0] + tc0 + uc1 + uc3, b0[0] + tb0]).astype(BF16)


def exchange_device(
    tokens,
    group_choice,
    members,
    route_weight,
    expert_home,
    expert_gate,
    expert_up,
    expert_down,
    shared_gate,
    shared_up,
    shared_down,
):
    node_count = lax.axis_size("node")
    local_count = lax.axis_size("local")
    device_count = node_count * local_count
    tok_rows, model_width = tokens.shape
    top_count = members.shape[1]
    experts_all = expert_home.shape[0]
    per_group = experts_all // GROUPS
    capacity = 2 * tok_rows * top_count // experts_all
    chosen = jnp.repeat(group_choice, 2, axis=1) * per_group + members
    onehot = (chosen[:, :, None] == jnp.arange(experts_all, dtype=jnp.int32)[None, None, :]).astype(
        jnp.int32
    )
    target = jnp.sum(onehot * expert_home[None, None, :], axis=-1)
    flat_hits = onehot.reshape(tok_rows * top_count, experts_all)
    before = jnp.cumsum(flat_hits, axis=0) - flat_hits
    position = jnp.sum(before * flat_hits, axis=-1).reshape(tok_rows, top_count)
    keep_mask = position < capacity
    slot_index = jnp.where(keep_mask, target * capacity + position, device_count * capacity)
    token_id = jnp.broadcast_to(
        jnp.arange(tok_rows, dtype=jnp.int32)[:, None], (tok_rows, top_count)
    )
    source_row = (
        jnp.full((device_count * capacity,), tok_rows, jnp.int32)
        .at[slot_index.reshape(-1)]
        .set(token_id.reshape(-1), mode="drop")
    )
    padded = jnp.concatenate([tokens, jnp.zeros((1, model_width), tokens.dtype)], axis=0)
    outgoing = padded[source_row].reshape(device_count, capacity, model_width)
    local_gate = expert_gate[0]
    local_up = expert_up[0]
    local_down = expert_down[0]
    arrived = lax.all_to_all(outgoing, ("node", "local"), split_axis=0, concat_axis=0, tiled=True)
    block_shape = arrived.shape
    row_block = arrived.reshape(-1, model_width)
    gate_part = jnp.dot(row_block, local_gate, preferred_element_type=jnp.float32)
    up_part = jnp.dot(row_block, local_up, preferred_element_type=jnp.float32)
    hidden = (jax.nn.silu(gate_part) * up_part).astype(jnp.bfloat16)
    result = jnp.dot(hidden, local_down, preferred_element_type=jnp.float32).astype(jnp.bfloat16)
    answered = lax.all_to_all(
        result.reshape(block_shape), ("node", "local"), split_axis=0, concat_axis=0, tiled=True
    )
    answered = answered.reshape(device_count * capacity, model_width)
    picked = answered[jnp.minimum(slot_index, device_count * capacity - 1)]
    weight = jnp.where(keep_mask, route_weight, 0.0)
    routed = jnp.zeros((tok_rows, model_width), jnp.float32)
    for choice_index in range(top_count):
        routed = routed + weight[:, choice_index, None] * picked[:, choice_index].astype(
            jnp.float32
        )
    node_rows = lax.all_gather(tokens, "local", axis=0, tiled=True)
    shared_hidden = (
        jax.nn.silu(jnp.dot(node_rows, shared_gate, preferred_element_type=jnp.float32))
        * jnp.dot(node_rows, shared_up, preferred_element_type=jnp.float32)
    ).astype(jnp.bfloat16)
    shared_part = lax.psum_scatter(
        jnp.dot(shared_hidden, shared_down, preferred_element_type=jnp.float32),
        "local",
        scatter_dimension=0,
        tiled=True,
    )
    return (routed + shared_part).astype(jnp.bfloat16)


def solution(mesh):
    in_specs = (
        P(("node", "local"), None),
        P(("node", "local"), None),
        P(("node", "local"), None),
        P(("node", "local"), None),
        P(),
        P(("node", "local"), None, None),
        P(("node", "local"), None, None),
        P(("node", "local"), None, None),
        P(None, "local"),
        P(None, "local"),
        P("local", None),
    )
    out_specs = P(("node", "local"), None)
    whole_gather = mesh.shape["node"] == 2 * Z_COUNT and mesh.shape["local"] == 4
    return jax.shard_map(
        block_device if whole_gather else exchange_device,
        mesh=mesh,
        in_specs=in_specs,
        out_specs=out_specs,
        check_vma=False,
    )
```

```python
import functools

import jax
import jax.numpy as jnp
from jax import lax
from jax.experimental import pallas as pl
from jax.experimental.pallas import tpu as pltpu
from jax.sharding import PartitionSpec as P

GROUPS = 8
AXES = ("node", "local")
F32 = jnp.float32
BF16 = jnp.bfloat16

Z_COUNT = 4


def permutation(move):
    pairs = []
    for z in range(Z_COUNT):
        for y in range(2):
            for x in range(2):
                for core in range(2):
                    to_z, to_y, to_x, to_core = move(z, y, x, core)
                    pairs.append(
                        (
                            ((z * 2 + y) * 2 + x) * 2 + core,
                            (((to_z % Z_COUNT) * 2 + to_y) * 2 + to_x) * 2 + to_core,
                        )
                    )
    return pairs


CORE = permutation(lambda z, y, x, core: (z, y, x, 1 - core))
ALONG_X = permutation(lambda z, y, x, core: (z, y, 1 - x, core))
ALONG_Y = permutation(lambda z, y, x, core: (z, 1 - y, x, core))
Z_UP = permutation(lambda z, y, x, core: (z + 1, y, x, core))
Z_DOWN = permutation(lambda z, y, x, core: (z - 1, y, x, core))
Z_DOWN_TWICE = permutation(lambda z, y, x, core: (z - 2, y, x, core))


def send(value, pairs):
    return lax.ppermute(value, AXES, pairs)


def join(*values):
    return jnp.concatenate(values, axis=0)


def barrier(*values):
    return lax.optimization_barrier(values)


def expert_kernel(
    base, shared, capacity, weight_ref, own_hbm, other_hbm, gate_hbm, up_hbm, down_hbm, *rest
):
    if shared:
        sgate_hbm, sup_hbm, sdown_hbm = rest[:3]
        rest = rest[3:]
    own_out, other_out, held, gate, up, down, rows, hidden, answers, totals = rest[:10]
    rest = rest[10:]
    if shared:
        sgate, sup, sdown, shidden = rest[:4]
        rest = rest[4:]
    token_sem, gate_sem, up_sem, down_sem, out_sem = rest[:5]
    source_count = 8
    tokens, width = held.shape[1:]
    inner = gate.shape[1]
    tile, out_tile = UP_TILE, DOWN_TILE

    copies = []
    for index in range(source_count):
        copies.append(
            pltpu.make_async_copy(
                (own_hbm, other_hbm)[index // 4].at[base + index % 4], held.at[index], token_sem.at[index]
            )
        )
    up_copies, down_copies = [], []
    for step in range(inner // tile):
        columns = pl.ds(step * tile, tile)
        up_copies.append(
            (
                pltpu.make_async_copy(gate_hbm.at[0, :, columns], gate.at[:, columns], gate_sem.at[step]),
                pltpu.make_async_copy(up_hbm.at[0, :, columns], up.at[:, columns], up_sem.at[step]),
            )
        )
    for step in range(width // out_tile):
        columns = pl.ds(step * out_tile, out_tile)
        down_copies.append(
            pltpu.make_async_copy(down_hbm.at[0, :, columns], down.at[:, columns], down_sem.at[step])
        )
    shared_copies = []
    if shared:
        shared_sem = rest[5]
        for number, (source, target) in enumerate(
            ((sgate_hbm, sgate), (sup_hbm, sup), (sdown_hbm, sdown))
        ):
            shared_copies.append(pltpu.make_async_copy(source, target, shared_sem.at[number]))
    waiting = [copy for pair in up_copies for copy in pair] + shared_copies + down_copies

    def start_more(count):
        for _ in range(min(count, len(waiting))):
            waiting.pop(0).start()

    for copy in copies:
        copy.start()
    start_more(2)

    weights = weight_ref[...]
    hits = (weights > 0.0).astype(BF16)
    earlier = (
        lax.broadcasted_iota(jnp.int32, (tokens, tokens), 0)
        < lax.broadcasted_iota(jnp.int32, (tokens, tokens), 1)
    ).astype(BF16)
    place = jnp.dot(hits, earlier, preferred_element_type=F32).astype(jnp.int32)
    slots = lax.broadcasted_iota(jnp.int32, (capacity, tokens), 0)
    for index in range(source_count):
        chosen = (place[index : index + 1] == slots) & (weights[index : index + 1] > 0.0)
        copies[index].wait()
        if index == source_count // 2:
            start_more(2)
        rows[pl.ds(index * capacity, capacity)] = jnp.dot(
            chosen.astype(BF16), held[index], preferred_element_type=F32
        ).astype(BF16)

    for step in range(inner // tile):
        columns = pl.ds(step * tile, tile)
        up_copies[step][0].wait()
        up_copies[step][1].wait()
        start_more(3)
        gate_part = jnp.dot(rows[...], gate[:, columns], preferred_element_type=F32)
        up_part = jnp.dot(rows[...], up[:, columns], preferred_element_type=F32)
        hidden[:, columns] = (gate_part / (1.0 + jnp.exp(-gate_part)) * up_part).astype(BF16)

    start_more(len(waiting))
    if shared:
        shared_copies[0].wait()
        shared_copies[1].wait()
        shared_copies[2].wait()
        shared_rows = jnp.concatenate([held[index] for index in SHARED_SOURCES], axis=0)
        gate_part = jnp.dot(shared_rows, sgate[...], preferred_element_type=F32)
        up_part = jnp.dot(shared_rows, sup[...], preferred_element_type=F32)
        shidden[...] = (gate_part / (1.0 + jnp.exp(-gate_part)) * up_part).astype(BF16)

    out_copies = []
    for step in range(width // out_tile):
        columns = pl.ds(step * out_tile, out_tile)
        down_copies[step].wait()
        answers[...] = jnp.dot(
            hidden[...], down[:, columns], preferred_element_type=F32
        ).astype(BF16)
        for index in range(source_count):
            weight_row = weights[index : index + 1]
            chosen = (place[index : index + 1] == slots) & (weight_row > 0.0)
            spread = jnp.where(chosen, jnp.broadcast_to(weight_row, chosen.shape), 0.0)
            high = spread.astype(BF16)
            low = (spread - high.astype(F32)).astype(BF16)
            answer = answers[pl.ds(index * capacity, capacity)]
            total = lax.dot_general(
                jnp.concatenate([high, low], axis=0),
                jnp.concatenate([answer, answer], axis=0),
                (((0,), (0,)), ((), ())),
                preferred_element_type=F32,
            )
            if shared and index in SHARED_SOURCES:
                total = total + jnp.dot(
                    shidden[pl.ds(SHARED_SOURCES.index(index) * tokens, tokens)],
                    sdown[:, columns],
                    preferred_element_type=F32,
                )
            totals[index, :, columns] = total.astype(BF16)
        for side, target in enumerate((own_out, other_out)):
            copy = pltpu.make_async_copy(
                totals.at[pl.ds(side * 4, 4), :, columns],
                target.at[:, :, columns],
                out_sem.at[step * 2 + side],
            )
            copy.start()
            out_copies.append(copy)
    for copy in out_copies:
        copy.wait()


UP_TILE = 256
DOWN_TILE = 512


SHARED_SOURCES = (0, 1, 4, 5)
VMEM_LIMIT = 44 * 1024 * 1024
FLOPS = 1000


def expert_chunk(weights, own, other, base, expert_weights, shared_weights, capacity):
    _, tokens, width = own.shape
    source_count = 8
    inner = expert_weights[0].shape[2]
    up_steps, down_steps = inner // UP_TILE, width // DOWN_TILE
    scratch = [
        pltpu.VMEM((source_count, tokens, width), BF16),
        pltpu.VMEM((width, inner), BF16),
        pltpu.VMEM((width, inner), BF16),
        pltpu.VMEM((inner, width), BF16),
        pltpu.VMEM((source_count * capacity, width), BF16),
        pltpu.VMEM((source_count * capacity, inner), BF16),
        pltpu.VMEM((source_count * capacity, DOWN_TILE), BF16),
        pltpu.VMEM((source_count, tokens, width), BF16),
    ]
    if shared_weights:
        shared_width = shared_weights[0].shape[1]
        scratch += [
            pltpu.VMEM((width, shared_width), BF16),
            pltpu.VMEM((width, shared_width), BF16),
            pltpu.VMEM((shared_width, width), BF16),
            pltpu.VMEM((len(SHARED_SOURCES) * tokens, shared_width), BF16),
        ]
    counts = (source_count, up_steps, up_steps, down_steps, 2 * down_steps)
    scratch += [pltpu.SemaphoreType.DMA((count,)) for count in counts]
    if shared_weights:
        scratch.append(pltpu.SemaphoreType.DMA((3,)))
    operands = (weights, own, other, *expert_weights, *shared_weights)
    return pl.pallas_call(
        functools.partial(expert_kernel, base, len(shared_weights) > 0, capacity),
        out_shape=[jax.ShapeDtypeStruct((4, tokens, width), BF16)] * 2,
        in_specs=[pl.BlockSpec(memory_space=pltpu.VMEM)]
        + [pl.BlockSpec(memory_space=pl.ANY)] * (len(operands) - 1),
        out_specs=[pl.BlockSpec(memory_space=pl.ANY)] * 2,
        scratch_shapes=scratch,
        cost_estimate=pl.CostEstimate(flops=FLOPS, bytes_accessed=FLOPS, transcendentals=0),
        compiler_params=pltpu.CompilerParams(vmem_limit_bytes=VMEM_LIMIT),
    )(*operands)


def assemble_kernel(count, *refs):
    c_near, c_far, b_near, b_far = refs[:4]
    parts_a, out, semaphore = refs[4 : 4 + count], refs[4 + count], refs[5 + count]
    rows_c, rows_b = c_near.shape[1], b_near.shape[1]
    only_c, only_b = pl.ds(0, rows_c), pl.ds(rows_c, rows_b)
    only_a = pl.ds(rows_c + rows_b, out.shape[1] - rows_c - rows_b)
    moves = []
    for k in range(count):
        moves.append((c_near.at[pl.ds(2 * k, 2)], out.at[pl.ds(4 * k, 2), only_c]))
        moves.append((c_far.at[pl.ds(2 * k, 2)], out.at[pl.ds(4 * k + 2, 2), only_c]))
        moves.append((parts_a[k], out.at[pl.ds(4 * k, 4), only_a]))
        for y in range(2):
            moves.append((b_near.at[2 * k + y], out.at[4 * k + 2 * y, only_b]))
            moves.append((b_far.at[2 * k + y], out.at[4 * k + 2 * y + 1, only_b]))
    copies = [
        pltpu.make_async_copy(source, target, semaphore.at[number])
        for number, (source, target) in enumerate(moves)
    ]
    for copy in copies:
        copy.start()
    for copy in copies:
        copy.wait()


def assemble(c_near, c_far, b_near, b_far, parts_a):
    count, width = len(parts_a), c_near.shape[2]
    tokens = c_near.shape[1] + b_near.shape[1] + parts_a[0].shape[1]
    return pl.pallas_call(
        functools.partial(assemble_kernel, count),
        out_shape=jax.ShapeDtypeStruct((4 * count, tokens, width), BF16),
        in_specs=[pl.BlockSpec(memory_space=pl.ANY)] * (4 + count),
        out_specs=pl.BlockSpec(memory_space=pl.ANY),
        scratch_shapes=[pltpu.SemaphoreType.DMA((7 * count,))],
        cost_estimate=pl.CostEstimate(flops=0, bytes_accessed=8 * count * tokens * width, transcendentals=0),
        compiler_params=pltpu.CompilerParams(vmem_limit_bytes=VMEM_LIMIT),
    )(c_near, c_far, b_near, b_far, *parts_a)


def route_table(group_choice, members, route_weight, expert_home, capacity):
    tok_rows = members.shape[0]
    experts_all = expert_home.shape[0]
    per_group = experts_all // GROUPS
    chosen = jnp.repeat(group_choice, 2, axis=1) * per_group + members
    ids = jnp.arange(experts_all, dtype=jnp.int32)
    target = jnp.sum(
        jnp.where(chosen[:, :, None] == ids[None, None, :], expert_home[None, None, :], 0), axis=-1
    )
    table = jnp.sum(
        jnp.where(target[:, :, None] == ids[None, None, :], route_weight[:, :, None], 0.0), axis=1
    )
    hits = (table > 0.0).astype(BF16)
    earlier = (
        lax.broadcasted_iota(jnp.int32, (tok_rows, tok_rows), 0)
        > lax.broadcasted_iota(jnp.int32, (tok_rows, tok_rows), 1)
    ).astype(BF16)
    place = jnp.dot(earlier, hits, preferred_element_type=F32)
    table = jnp.where(place < capacity, table, 0.0)
    return table.T


def block_device(
    tokens,
    group_choice,
    members,
    route_weight,
    expert_home,
    expert_gate,
    expert_up,
    expert_down,
    shared_gate,
    shared_up,
    shared_down,
):
    tok_rows, width = tokens.shape
    experts_all = expert_home.shape[0]
    capacity = 2 * tok_rows * members.shape[1] // experts_all
    expert_weights = (expert_gate, expert_up, expert_down)
    shared_weights = (shared_gate, shared_up, shared_down)

    rows_c, rows_b = tok_rows // 2, tok_rows * 3 // 8
    c = tokens[None, :rows_c]
    b = tokens[None, rows_c : rows_c + rows_b]
    a = tokens[None, rows_c + rows_b :]
    table = route_table(group_choice, members, route_weight, expert_home, capacity)

    c1, c3, cx0, ax, by = (
        send(c, Z_UP),
        send(c, Z_DOWN),
        send(c, ALONG_X),
        send(a, ALONG_X),
        send(b, ALONG_Y),
    )
    c, b, a, c1, c3, cx0, ax, by, table = barrier(c, b, a, c1, c3, cx0, ax, by, table)

    b0, c0, a0 = join(b, by), join(c, cx0), join(a, ax)
    c13 = join(c1, c3)
    b1, b3, cy0, bx0, cx13, c2, ay = (
        send(b0, Z_UP),
        send(b0, Z_DOWN),
        send(c0, ALONG_Y),
        send(b0, ALONG_X),
        send(c13, ALONG_X),
        send(c1, Z_UP),
        send(a0, ALONG_Y),
    )
    received = lax.all_to_all(table, AXES, split_axis=0, concat_axis=0, tiled=True)
    c0, b0, a0, c13, c2, b1, b3, cx13, bx0, cy0, ay, received = barrier(
        c0, b0, a0, c13, c2, b1, b3, cx13, bx0, cy0, ay, received
    )

    node, local = lax.axis_index("node"), lax.axis_index("local")
    z, y, x, core = node // 2, node % 2, local // 2, local % 2
    order = []
    for far_z in range(Z_COUNT):
        for far_core in range(2):
            for far_y in range(2):
                for far_x in range(2):
                    source = ((z - far_z) % Z_COUNT * 2 + (y ^ far_y)) * 2 + (x ^ far_x)
                    order.append(source * 2 + (core ^ far_core))
    weights = jnp.take(received, jnp.stack(order), axis=0)

    def expert(k, own, other, base=0):
        shared = shared_weights if k == 0 else ()
        return expert_chunk(
            weights[k * 8 : k * 8 + 8], own, other, base, expert_weights, shared, capacity
        )

    a0 = join(a0, ay)
    b13 = join(b1, b3)
    c13 = jnp.concatenate([c13[0], cx13[0], c13[1], cx13[1]]).reshape(4, rows_c, width)
    whole0 = assemble(c0, cy0, b0, bx0, (a0,))
    other0, cy13, bx13, b2, a1, cx2, a3 = (
        send(whole0, CORE),
        send(c13, ALONG_Y),
        send(b13, ALONG_X),
        send(b1, Z_UP),
        send(a0, Z_UP),
        send(c2, ALONG_X),
        send(a0, Z_DOWN),
    )
    own0, far0 = expert(0, whole0, other0)
    c13, b13, c2, b2, a1, a3, cx2, bx13, cy13, own0, far0 = barrier(
        c13, b13, c2, b2, a1, a3, cx2, bx13, cy13, own0, far0
    )

    rows_yx = tok_rows * 5 // 8
    only_c, only_b = slice(0, rows_yx), slice(rows_yx, None)
    near_y, far_y, near_x, far_x = slice(0, 2), slice(2, 4), slice(0, 4, 2), slice(1, 4, 2)

    def total(pair, blocks, part):
        return pair[0][blocks, part].astype(F32) + pair[1][blocks, part].astype(F32)

    def back(value, pairs):
        return send(value.astype(BF16), pairs)

    c2 = join(c2, cx2)
    whole13 = assemble(c13, cy13, b13, bx13, (a1, a3))
    back0, cy2, bx2, a2, other13 = (
        send(far0, CORE),
        send(c2, ALONG_Y),
        send(b2, ALONG_X),
        send(a1, Z_UP),
        send(whole13, CORE),
    )
    pair0 = (own0, back0)
    sc0 = back(total(pair0, far_y, only_c), ALONG_Y)
    sb0 = back(total(pair0, far_x, only_b), ALONG_X)
    own1, far1 = expert(1, whole13, other13)
    c2, b2, a2, bx2, cy2, other13, whole13, own1, far1, sc0, sb0 = barrier(
        c2, b2, a2, bx2, cy2, other13, whole13, own1, far1, sc0, sb0
    )

    whole2 = assemble(c2, cy2, b2, bx2, (a2,))
    other2, back1 = send(whole2, CORE), send(far1, CORE)
    pair1 = (own1, back1)
    sc1 = total(pair1, far_y, only_c).astype(BF16)
    sb1 = total(pair1, far_x, only_b).astype(BF16)
    sc1, sb1, whole2, other2 = barrier(sc1, sb1, whole2, other2)
    sc1, sb1 = send(sc1, ALONG_Y), send(sb1, ALONG_X)
    own2, far2 = expert(2, whole2, other2)
    sc1, sb1, own2, far2 = barrier(sc1, sb1, own2, far2)
    back2 = send(far2, CORE)
    pair2 = (own2, back2)
    sc2 = total(pair2, far_y, only_c).astype(BF16)
    sb2 = total(pair2, far_x, only_b).astype(BF16)
    c1 = total(pair1, near_y, only_c) + sc1
    tc1 = c1[1].astype(BF16)
    tb1 = (total(pair1, near_x, only_b) + sb1).astype(BF16)
    sc2, sb2, tc1, tb1, whole13, other13 = barrier(sc2, sb2, tc1, tb1, whole13, other13)

    sc2, sb2, tc1 = send(sc2, ALONG_Y), send(sb2, ALONG_X), send(tc1, ALONG_X)
    tb1 = send(tb1, Z_DOWN)
    own3, far3 = expert(3, whole13, other13, 4)
    own3, far3, sb2, sc2, tc1, tb1 = barrier(own3, far3, sb2, sc2, tc1, tb1)

    back3 = send(far3, CORE)
    c2 = total(pair2, near_y, only_c) + sc2
    b2 = total(pair2, near_x, only_b) + sb2
    pair3 = (own3, back3)
    tb2, tc2, sc3, sb3 = (
        back(b2, Z_DOWN_TWICE),
        back(c2[1], ALONG_X),
        back(total(pair3, far_y, only_c), ALONG_Y),
        back(total(pair3, far_x, only_b), ALONG_X),
    )
    tb2, tc2, sb3, sc3 = barrier(tb2, tc2, sb3, sc3)

    c2 = c2[0] + tc2
    b3 = total(pair3, near_x, only_b) + sb3
    c3 = total(pair3, near_y, only_c) + sc3
    c0 = total(pair0, near_y, only_c) + sc0
    tb3, uc2, tc3, tc0 = (
        back(b3, Z_UP),
        back(c2, Z_DOWN),
        back(c3[1], ALONG_X),
        back(c0[1], ALONG_X),
    )
    uc2, tb3, tc3, tc0 = barrier(uc2, tb3, tc3, tc0)

    c1 = c1[0] + tc1 + uc2
    c3 = c3[0] + tc3
    b0 = total(pair0, near_x, only_b) + sb0 + tb1 + tb2 + tb3
    uc1, uc3, tb0 = back(c1, Z_DOWN), back(c3, Z_UP), back(b0[1], ALONG_Y)
    return jnp.concatenate([c0[0] + tc0 + uc1 + uc3, b0[0] + tb0]).astype(BF16)


def exchange_device(
    tokens,
    group_choice,
    members,
    route_weight,
    expert_home,
    expert_gate,
    expert_up,
    expert_down,
    shared_gate,
    shared_up,
    shared_down,
):
    node_count = lax.axis_size("node")
    local_count = lax.axis_size("local")
    device_count = node_count * local_count
    tok_rows, model_width = tokens.shape
    top_count = members.shape[1]
    experts_all = expert_home.shape[0]
    per_group = experts_all // GROUPS
    capacity = 2 * tok_rows * top_count // experts_all
    chosen = jnp.repeat(group_choice, 2, axis=1) * per_group + members
    onehot = (chosen[:, :, None] == jnp.arange(experts_all, dtype=jnp.int32)[None, None, :]).astype(
        jnp.int32
    )
    target = jnp.sum(onehot * expert_home[None, None, :], axis=-1)
    flat_hits = onehot.reshape(tok_rows * top_count, experts_all)
    before = jnp.cumsum(flat_hits, axis=0) - flat_hits
    position = jnp.sum(before * flat_hits, axis=-1).reshape(tok_rows, top_count)
    keep_mask = position < capacity
    slot_index = jnp.where(keep_mask, target * capacity + position, device_count * capacity)
    token_id = jnp.broadcast_to(
        jnp.arange(tok_rows, dtype=jnp.int32)[:, None], (tok_rows, top_count)
    )
    source_row = (
        jnp.full((device_count * capacity,), tok_rows, jnp.int32)
        .at[slot_index.reshape(-1)]
        .set(token_id.reshape(-1), mode="drop")
    )
    padded = jnp.concatenate([tokens, jnp.zeros((1, model_width), tokens.dtype)], axis=0)
    outgoing = padded[source_row].reshape(device_count, capacity, model_width)
    local_gate = expert_gate[0]
    local_up = expert_up[0]
    local_down = expert_down[0]
    arrived = lax.all_to_all(outgoing, ("node", "local"), split_axis=0, concat_axis=0, tiled=True)
    block_shape = arrived.shape
    row_block = arrived.reshape(-1, model_width)
    gate_part = jnp.dot(row_block, local_gate, preferred_element_type=jnp.float32)
    up_part = jnp.dot(row_block, local_up, preferred_element_type=jnp.float32)
    hidden = (jax.nn.silu(gate_part) * up_part).astype(jnp.bfloat16)
    result = jnp.dot(hidden, local_down, preferred_element_type=jnp.float32).astype(jnp.bfloat16)
    answered = lax.all_to_all(
        result.reshape(block_shape), ("node", "local"), split_axis=0, concat_axis=0, tiled=True
    )
    answered = answered.reshape(device_count * capacity, model_width)
    picked = answered[jnp.minimum(slot_index, device_count * capacity - 1)]
    weight = jnp.where(keep_mask, route_weight, 0.0)
    routed = jnp.zeros((tok_rows, model_width), jnp.float32)
    for choice_index in range(top_count):
        routed = routed + weight[:, choice_index, None] * picked[:, choice_index].astype(
            jnp.float32
        )
    node_rows = lax.all_gather(tokens, "local", axis=0, tiled=True)
    shared_hidden = (
        jax.nn.silu(jnp.dot(node_rows, shared_gate, preferred_element_type=jnp.float32))
        * jnp.dot(node_rows, shared_up, preferred_element_type=jnp.float32)
    ).astype(jnp.bfloat16)
    shared_part = lax.psum_scatter(
        jnp.dot(shared_hidden, shared_down, preferred_element_type=jnp.float32),
        "local",
        scatter_dimension=0,
        tiled=True,
    )
    return (routed + shared_part).astype(jnp.bfloat16)


def solution(mesh):
    in_specs = (
        P(("node", "local"), None),
        P(("node", "local"), None),
        P(("node", "local"), None),
        P(("node", "local"), None),
        P(),
        P(("node", "local"), None, None),
        P(("node", "local"), None, None),
        P(("node", "local"), None, None),
        P(None, "local"),
        P(None, "local"),
        P("local", None),
    )
    out_specs = P(("node", "local"), None)
    whole_gather = mesh.shape["node"] == 2 * Z_COUNT and mesh.shape["local"] == 4
    return jax.shard_map(
        block_device if whole_gather else exchange_device,
        mesh=mesh,
        in_specs=in_specs,
        out_specs=out_specs,
        check_vma=False,
    )
```

```python
import functools

import jax
import jax.numpy as jnp
from jax import lax
from jax.experimental import pallas as pl
from jax.experimental.pallas import tpu as pltpu
from jax.sharding import PartitionSpec as P

GROUPS = 8
AXES = ("node", "local")
F32 = jnp.float32
BF16 = jnp.bfloat16

Z_COUNT = 4


def permutation(move):
    pairs = []
    for z in range(Z_COUNT):
        for y in range(2):
            for x in range(2):
                for core in range(2):
                    to_z, to_y, to_x, to_core = move(z, y, x, core)
                    pairs.append(
                        (
                            ((z * 2 + y) * 2 + x) * 2 + core,
                            (((to_z % Z_COUNT) * 2 + to_y) * 2 + to_x) * 2 + to_core,
                        )
                    )
    return pairs


CORE = permutation(lambda z, y, x, core: (z, y, x, 1 - core))
ALONG_X = permutation(lambda z, y, x, core: (z, y, 1 - x, core))
ALONG_Y = permutation(lambda z, y, x, core: (z, 1 - y, x, core))
Z_UP = permutation(lambda z, y, x, core: (z + 1, y, x, core))
Z_DOWN = permutation(lambda z, y, x, core: (z - 1, y, x, core))
Z_DOWN_TWICE = permutation(lambda z, y, x, core: (z - 2, y, x, core))


def send(value, pairs):
    return lax.ppermute(value, AXES, pairs)


def join(*values):
    return jnp.concatenate(values, axis=0)


def barrier(*values):
    return lax.optimization_barrier(values)


def expert_kernel(
    base, shared, capacity, weight_ref, own_hbm, other_hbm, gate_hbm, up_hbm, down_hbm, *rest
):
    if shared:
        sgate_hbm, sup_hbm, sdown_hbm = rest[:3]
        rest = rest[3:]
    own_out, other_out, held, gate, up, down, rows, hidden, answers, totals = rest[:10]
    rest = rest[10:]
    if shared:
        sgate, sup, sdown, shidden = rest[:4]
        rest = rest[4:]
    token_sem, gate_sem, up_sem, down_sem, out_sem = rest[:5]
    source_count = 8
    tokens, width = held.shape[1:]
    inner = gate.shape[1]
    tile, out_tile = UP_TILE, DOWN_TILE

    copies = []
    for index in range(source_count):
        copies.append(
            pltpu.make_async_copy(
                (own_hbm, other_hbm)[index // 4].at[base + index % 4], held.at[index], token_sem.at[index]
            )
        )
    gate_copy = pltpu.make_async_copy(gate_hbm.at[0], gate, gate_sem.at[0])
    up_copy = pltpu.make_async_copy(up_hbm.at[0], up, up_sem.at[0])
    down_copy = pltpu.make_async_copy(down_hbm.at[0], down, down_sem.at[0])
    shared_copies = []
    if shared:
        shared_sem = rest[5]
        for number, (source, target) in enumerate(
            ((sgate_hbm, sgate), (sup_hbm, sup), (sdown_hbm, sdown))
        ):
            shared_copies.append(pltpu.make_async_copy(source, target, shared_sem.at[number]))
    for copy in copies:
        copy.start()
    gate_copy.start()

    weights = weight_ref[...]
    hits = (weights > 0.0).astype(BF16)
    earlier = (
        lax.broadcasted_iota(jnp.int32, (tokens, tokens), 0)
        < lax.broadcasted_iota(jnp.int32, (tokens, tokens), 1)
    ).astype(BF16)
    place = jnp.dot(hits, earlier, preferred_element_type=F32).astype(jnp.int32)
    slots = lax.broadcasted_iota(jnp.int32, (capacity, tokens), 0)
    for index in range(source_count):
        chosen = (place[index : index + 1] == slots) & (weights[index : index + 1] > 0.0)
        copies[index].wait()
        if index == source_count // 2:
            up_copy.start()
        rows[pl.ds(index * capacity, capacity)] = jnp.dot(
            chosen.astype(BF16), held[index], preferred_element_type=F32
        ).astype(BF16)

    gate_copy.wait()
    up_copy.wait()
    for copy in shared_copies:
        copy.start()
    down_copy.start()
    for step in range(inner // tile):
        columns = pl.ds(step * tile, tile)
        gate_part = jnp.dot(rows[...], gate[:, columns], preferred_element_type=F32)
        up_part = jnp.dot(rows[...], up[:, columns], preferred_element_type=F32)
        hidden[:, columns] = (gate_part / (1.0 + jnp.exp(-gate_part)) * up_part).astype(BF16)

    if shared:
        shared_copies[0].wait()
        shared_copies[1].wait()
        shared_copies[2].wait()
        shared_rows = jnp.concatenate([held[index] for index in SHARED_SOURCES], axis=0)
        gate_part = jnp.dot(shared_rows, sgate[...], preferred_element_type=F32)
        up_part = jnp.dot(shared_rows, sup[...], preferred_element_type=F32)
        shidden[...] = (gate_part / (1.0 + jnp.exp(-gate_part)) * up_part).astype(BF16)

    down_copy.wait()
    out_copies = []
    for step in range(width // out_tile):
        columns = pl.ds(step * out_tile, out_tile)
        answers[...] = jnp.dot(
            hidden[...], down[:, columns], preferred_element_type=F32
        ).astype(BF16)
        for index in range(source_count):
            weight_row = weights[index : index + 1]
            chosen = (place[index : index + 1] == slots) & (weight_row > 0.0)
            spread = jnp.where(chosen, jnp.broadcast_to(weight_row, chosen.shape), 0.0)
            high = spread.astype(BF16)
            low = (spread - high.astype(F32)).astype(BF16)
            answer = answers[pl.ds(index * capacity, capacity)]
            total = lax.dot_general(
                jnp.concatenate([high, low], axis=0),
                jnp.concatenate([answer, answer], axis=0),
                (((0,), (0,)), ((), ())),
                preferred_element_type=F32,
            )
            if shared and index in SHARED_SOURCES:
                total = total + jnp.dot(
                    shidden[pl.ds(SHARED_SOURCES.index(index) * tokens, tokens)],
                    sdown[:, columns],
                    preferred_element_type=F32,
                )
            totals[index, :, columns] = total.astype(BF16)
        for side, target in enumerate((own_out, other_out)):
            copy = pltpu.make_async_copy(
                totals.at[pl.ds(side * 4, 4), :, columns],
                target.at[:, :, columns],
                out_sem.at[step * 2 + side],
            )
            copy.start()
            out_copies.append(copy)
    for copy in out_copies:
        copy.wait()


UP_TILE = 256
DOWN_TILE = 512


SHARED_SOURCES = (0, 1, 4, 5)
VMEM_LIMIT = 44 * 1024 * 1024
FLOPS = 1000


def expert_chunk(weights, own, other, base, expert_weights, shared_weights, capacity):
    _, tokens, width = own.shape
    source_count = 8
    inner = expert_weights[0].shape[2]
    down_steps = width // DOWN_TILE
    scratch = [
        pltpu.VMEM((source_count, tokens, width), BF16),
        pltpu.VMEM((width, inner), BF16),
        pltpu.VMEM((width, inner), BF16),
        pltpu.VMEM((inner, width), BF16),
        pltpu.VMEM((source_count * capacity, width), BF16),
        pltpu.VMEM((source_count * capacity, inner), BF16),
        pltpu.VMEM((source_count * capacity, DOWN_TILE), BF16),
        pltpu.VMEM((source_count, tokens, width), BF16),
    ]
    if shared_weights:
        shared_width = shared_weights[0].shape[1]
        scratch += [
            pltpu.VMEM((width, shared_width), BF16),
            pltpu.VMEM((width, shared_width), BF16),
            pltpu.VMEM((shared_width, width), BF16),
            pltpu.VMEM((len(SHARED_SOURCES) * tokens, shared_width), BF16),
        ]
    counts = (source_count, 1, 1, 1, 2 * down_steps)
    scratch += [pltpu.SemaphoreType.DMA((count,)) for count in counts]
    if shared_weights:
        scratch.append(pltpu.SemaphoreType.DMA((3,)))
    operands = (weights, own, other, *expert_weights, *shared_weights)
    return pl.pallas_call(
        functools.partial(expert_kernel, base, len(shared_weights) > 0, capacity),
        out_shape=[jax.ShapeDtypeStruct((4, tokens, width), BF16)] * 2,
        in_specs=[pl.BlockSpec(memory_space=pltpu.VMEM)]
        + [pl.BlockSpec(memory_space=pl.ANY)] * (len(operands) - 1),
        out_specs=[pl.BlockSpec(memory_space=pl.ANY)] * 2,
        scratch_shapes=scratch,
        cost_estimate=pl.CostEstimate(flops=FLOPS, bytes_accessed=FLOPS, transcendentals=0),
        compiler_params=pltpu.CompilerParams(vmem_limit_bytes=VMEM_LIMIT),
    )(*operands)


def assemble_kernel(count, *refs):
    c_near, c_far, b_near, b_far = refs[:4]
    parts_a, out, semaphore = refs[4 : 4 + count], refs[4 + count], refs[5 + count]
    rows_c, rows_b = c_near.shape[1], b_near.shape[1]
    only_c, only_b = pl.ds(0, rows_c), pl.ds(rows_c, rows_b)
    only_a = pl.ds(rows_c + rows_b, out.shape[1] - rows_c - rows_b)
    moves = []
    for k in range(count):
        moves.append((c_near.at[pl.ds(2 * k, 2)], out.at[pl.ds(4 * k, 2), only_c]))
        moves.append((c_far.at[pl.ds(2 * k, 2)], out.at[pl.ds(4 * k + 2, 2), only_c]))
        moves.append((parts_a[k], out.at[pl.ds(4 * k, 4), only_a]))
        for y in range(2):
            moves.append((b_near.at[2 * k + y], out.at[4 * k + 2 * y, only_b]))
            moves.append((b_far.at[2 * k + y], out.at[4 * k + 2 * y + 1, only_b]))
    copies = [
        pltpu.make_async_copy(source, target, semaphore.at[number])
        for number, (source, target) in enumerate(moves)
    ]
    for copy in copies:
        copy.start()
    for copy in copies:
        copy.wait()


def assemble(c_near, c_far, b_near, b_far, parts_a):
    count, width = len(parts_a), c_near.shape[2]
    tokens = c_near.shape[1] + b_near.shape[1] + parts_a[0].shape[1]
    return pl.pallas_call(
        functools.partial(assemble_kernel, count),
        out_shape=jax.ShapeDtypeStruct((4 * count, tokens, width), BF16),
        in_specs=[pl.BlockSpec(memory_space=pl.ANY)] * (4 + count),
        out_specs=pl.BlockSpec(memory_space=pl.ANY),
        scratch_shapes=[pltpu.SemaphoreType.DMA((7 * count,))],
        cost_estimate=pl.CostEstimate(flops=0, bytes_accessed=8 * count * tokens * width, transcendentals=0),
        compiler_params=pltpu.CompilerParams(vmem_limit_bytes=VMEM_LIMIT),
    )(c_near, c_far, b_near, b_far, *parts_a)


def route_table(group_choice, members, route_weight, expert_home, capacity):
    tok_rows = members.shape[0]
    experts_all = expert_home.shape[0]
    per_group = experts_all // GROUPS
    chosen = jnp.repeat(group_choice, 2, axis=1) * per_group + members
    ids = jnp.arange(experts_all, dtype=jnp.int32)
    target = jnp.sum(
        jnp.where(chosen[:, :, None] == ids[None, None, :], expert_home[None, None, :], 0), axis=-1
    )
    table = jnp.sum(
        jnp.where(target[:, :, None] == ids[None, None, :], route_weight[:, :, None], 0.0), axis=1
    )
    hits = (table > 0.0).astype(BF16)
    earlier = (
        lax.broadcasted_iota(jnp.int32, (tok_rows, tok_rows), 0)
        > lax.broadcasted_iota(jnp.int32, (tok_rows, tok_rows), 1)
    ).astype(BF16)
    place = jnp.dot(earlier, hits, preferred_element_type=F32)
    table = jnp.where(place < capacity, table, 0.0)
    return table.T


def block_device(
    tokens,
    group_choice,
    members,
    route_weight,
    expert_home,
    expert_gate,
    expert_up,
    expert_down,
    shared_gate,
    shared_up,
    shared_down,
):
    tok_rows, width = tokens.shape
    experts_all = expert_home.shape[0]
    capacity = 2 * tok_rows * members.shape[1] // experts_all
    expert_weights = (expert_gate, expert_up, expert_down)
    shared_weights = (shared_gate, shared_up, shared_down)

    rows_c, rows_b = tok_rows // 2, tok_rows * 3 // 8
    c = tokens[None, :rows_c]
    b = tokens[None, rows_c : rows_c + rows_b]
    a = tokens[None, rows_c + rows_b :]
    table = route_table(group_choice, members, route_weight, expert_home, capacity)

    c1, c3, cx0, ax, by = (
        send(c, Z_UP),
        send(c, Z_DOWN),
        send(c, ALONG_X),
        send(a, ALONG_X),
        send(b, ALONG_Y),
    )
    c, b, a, c1, c3, cx0, ax, by, table = barrier(c, b, a, c1, c3, cx0, ax, by, table)

    b0, c0, a0 = join(b, by), join(c, cx0), join(a, ax)
    c13 = join(c1, c3)
    b1, b3, cy0, bx0, cx13, c2, ay = (
        send(b0, Z_UP),
        send(b0, Z_DOWN),
        send(c0, ALONG_Y),
        send(b0, ALONG_X),
        send(c13, ALONG_X),
        send(c1, Z_UP),
        send(a0, ALONG_Y),
    )
    received = lax.all_to_all(table, AXES, split_axis=0, concat_axis=0, tiled=True)
    c0, b0, a0, c13, c2, b1, b3, cx13, bx0, cy0, ay, received = barrier(
        c0, b0, a0, c13, c2, b1, b3, cx13, bx0, cy0, ay, received
    )

    node, local = lax.axis_index("node"), lax.axis_index("local")
    z, y, x, core = node // 2, node % 2, local // 2, local % 2
    order = []
    for far_z in range(Z_COUNT):
        for far_core in range(2):
            for far_y in range(2):
                for far_x in range(2):
                    source = ((z - far_z) % Z_COUNT * 2 + (y ^ far_y)) * 2 + (x ^ far_x)
                    order.append(source * 2 + (core ^ far_core))
    weights = jnp.take(received, jnp.stack(order), axis=0)

    def expert(k, own, other, base=0):
        shared = shared_weights if k == 0 else ()
        return expert_chunk(
            weights[k * 8 : k * 8 + 8], own, other, base, expert_weights, shared, capacity
        )

    a0 = join(a0, ay)
    b13 = join(b1, b3)
    c13 = jnp.concatenate([c13[0], cx13[0], c13[1], cx13[1]]).reshape(4, rows_c, width)
    whole0 = assemble(c0, cy0, b0, bx0, (a0,))
    other0, cy13, bx13, b2, a1, cx2, a3 = (
        send(whole0, CORE),
        send(c13, ALONG_Y),
        send(b13, ALONG_X),
        send(b1, Z_UP),
        send(a0, Z_UP),
        send(c2, ALONG_X),
        send(a0, Z_DOWN),
    )
    own0, far0 = expert(0, whole0, other0)
    c13, b13, c2, b2, a1, a3, cx2, bx13, cy13, own0, far0 = barrier(
        c13, b13, c2, b2, a1, a3, cx2, bx13, cy13, own0, far0
    )

    rows_yx = tok_rows * 5 // 8
    only_c, only_b = slice(0, rows_yx), slice(rows_yx, None)
    near_y, far_y, near_x, far_x = slice(0, 2), slice(2, 4), slice(0, 4, 2), slice(1, 4, 2)

    def total(pair, blocks, part):
        return pair[0][blocks, part].astype(F32) + pair[1][blocks, part].astype(F32)

    def back(value, pairs):
        return send(value.astype(BF16), pairs)

    c2 = join(c2, cx2)
    whole13 = assemble(c13, cy13, b13, bx13, (a1, a3))
    back0, cy2, bx2, a2, other13 = (
        send(far0, CORE),
        send(c2, ALONG_Y),
        send(b2, ALONG_X),
        send(a1, Z_UP),
        send(whole13, CORE),
    )
    pair0 = (own0, back0)
    sc0 = back(total(pair0, far_y, only_c), ALONG_Y)
    sb0 = back(total(pair0, far_x, only_b), ALONG_X)
    own1, far1 = expert(1, whole13, other13)
    c2, b2, a2, bx2, cy2, other13, whole13, own1, far1, sc0, sb0 = barrier(
        c2, b2, a2, bx2, cy2, other13, whole13, own1, far1, sc0, sb0
    )

    whole2 = assemble(c2, cy2, b2, bx2, (a2,))
    other2, back1 = send(whole2, CORE), send(far1, CORE)
    pair1 = (own1, back1)
    sc1 = total(pair1, far_y, only_c).astype(BF16)
    sb1 = total(pair1, far_x, only_b).astype(BF16)
    sc1, sb1, whole2, other2 = barrier(sc1, sb1, whole2, other2)
    sc1, sb1 = send(sc1, ALONG_Y), send(sb1, ALONG_X)
    own2, far2 = expert(2, whole2, other2)
    sc1, sb1, own2, far2 = barrier(sc1, sb1, own2, far2)
    back2 = send(far2, CORE)
    pair2 = (own2, back2)
    sc2 = total(pair2, far_y, only_c).astype(BF16)
    sb2 = total(pair2, far_x, only_b).astype(BF16)
    c1 = total(pair1, near_y, only_c) + sc1
    tc1 = c1[1].astype(BF16)
    tb1 = (total(pair1, near_x, only_b) + sb1).astype(BF16)
    sc2, sb2, tc1, tb1, whole13, other13 = barrier(sc2, sb2, tc1, tb1, whole13, other13)

    sc2, sb2, tc1 = send(sc2, ALONG_Y), send(sb2, ALONG_X), send(tc1, ALONG_X)
    tb1 = send(tb1, Z_DOWN)
    own3, far3 = expert(3, whole13, other13, 4)
    own3, far3, sb2, sc2, tc1, tb1 = barrier(own3, far3, sb2, sc2, tc1, tb1)

    back3 = send(far3, CORE)
    c2 = total(pair2, near_y, only_c) + sc2
    b2 = total(pair2, near_x, only_b) + sb2
    pair3 = (own3, back3)
    tb2, tc2, sc3, sb3 = (
        back(b2, Z_DOWN_TWICE),
        back(c2[1], ALONG_X),
        back(total(pair3, far_y, only_c), ALONG_Y),
        back(total(pair3, far_x, only_b), ALONG_X),
    )
    tb2, tc2, sb3, sc3 = barrier(tb2, tc2, sb3, sc3)

    c2 = c2[0] + tc2
    b3 = total(pair3, near_x, only_b) + sb3
    c3 = total(pair3, near_y, only_c) + sc3
    c0 = total(pair0, near_y, only_c) + sc0
    tb3, uc2, tc3, tc0 = (
        back(b3, Z_UP),
        back(c2, Z_DOWN),
        back(c3[1], ALONG_X),
        back(c0[1], ALONG_X),
    )
    uc2, tb3, tc3, tc0 = barrier(uc2, tb3, tc3, tc0)

    c1 = c1[0] + tc1 + uc2
    c3 = c3[0] + tc3
    b0 = total(pair0, near_x, only_b) + sb0 + tb1 + tb2 + tb3
    uc1, uc3, tb0 = back(c1, Z_DOWN), back(c3, Z_UP), back(b0[1], ALONG_Y)
    return jnp.concatenate([c0[0] + tc0 + uc1 + uc3, b0[0] + tb0]).astype(BF16)


def exchange_device(
    tokens,
    group_choice,
    members,
    route_weight,
    expert_home,
    expert_gate,
    expert_up,
    expert_down,
    shared_gate,
    shared_up,
    shared_down,
):
    node_count = lax.axis_size("node")
    local_count = lax.axis_size("local")
    device_count = node_count * local_count
    tok_rows, model_width = tokens.shape
    top_count = members.shape[1]
    experts_all = expert_home.shape[0]
    per_group = experts_all // GROUPS
    capacity = 2 * tok_rows * top_count // experts_all
    chosen = jnp.repeat(group_choice, 2, axis=1) * per_group + members
    onehot = (chosen[:, :, None] == jnp.arange(experts_all, dtype=jnp.int32)[None, None, :]).astype(
        jnp.int32
    )
    target = jnp.sum(onehot * expert_home[None, None, :], axis=-1)
    flat_hits = onehot.reshape(tok_rows * top_count, experts_all)
    before = jnp.cumsum(flat_hits, axis=0) - flat_hits
    position = jnp.sum(before * flat_hits, axis=-1).reshape(tok_rows, top_count)
    keep_mask = position < capacity
    slot_index = jnp.where(keep_mask, target * capacity + position, device_count * capacity)
    token_id = jnp.broadcast_to(
        jnp.arange(tok_rows, dtype=jnp.int32)[:, None], (tok_rows, top_count)
    )
    source_row = (
        jnp.full((device_count * capacity,), tok_rows, jnp.int32)
        .at[slot_index.reshape(-1)]
        .set(token_id.reshape(-1), mode="drop")
    )
    padded = jnp.concatenate([tokens, jnp.zeros((1, model_width), tokens.dtype)], axis=0)
    outgoing = padded[source_row].reshape(device_count, capacity, model_width)
    local_gate = expert_gate[0]
    local_up = expert_up[0]
    local_down = expert_down[0]
    arrived = lax.all_to_all(outgoing, ("node", "local"), split_axis=0, concat_axis=0, tiled=True)
    block_shape = arrived.shape
    row_block = arrived.reshape(-1, model_width)
    gate_part = jnp.dot(row_block, local_gate, preferred_element_type=jnp.float32)
    up_part = jnp.dot(row_block, local_up, preferred_element_type=jnp.float32)
    hidden = (jax.nn.silu(gate_part) * up_part).astype(jnp.bfloat16)
    result = jnp.dot(hidden, local_down, preferred_element_type=jnp.float32).astype(jnp.bfloat16)
    answered = lax.all_to_all(
        result.reshape(block_shape), ("node", "local"), split_axis=0, concat_axis=0, tiled=True
    )
    answered = answered.reshape(device_count * capacity, model_width)
    picked = answered[jnp.minimum(slot_index, device_count * capacity - 1)]
    weight = jnp.where(keep_mask, route_weight, 0.0)
    routed = jnp.zeros((tok_rows, model_width), jnp.float32)
    for choice_index in range(top_count):
        routed = routed + weight[:, choice_index, None] * picked[:, choice_index].astype(
            jnp.float32
        )
    node_rows = lax.all_gather(tokens, "local", axis=0, tiled=True)
    shared_hidden = (
        jax.nn.silu(jnp.dot(node_rows, shared_gate, preferred_element_type=jnp.float32))
        * jnp.dot(node_rows, shared_up, preferred_element_type=jnp.float32)
    ).astype(jnp.bfloat16)
    shared_part = lax.psum_scatter(
        jnp.dot(shared_hidden, shared_down, preferred_element_type=jnp.float32),
        "local",
        scatter_dimension=0,
        tiled=True,
    )
    return (routed + shared_part).astype(jnp.bfloat16)


def solution(mesh):
    in_specs = (
        P(("node", "local"), None),
        P(("node", "local"), None),
        P(("node", "local"), None),
        P(("node", "local"), None),
        P(),
        P(("node", "local"), None, None),
        P(("node", "local"), None, None),
        P(("node", "local"), None, None),
        P(None, "local"),
        P(None, "local"),
        P("local", None),
    )
    out_specs = P(("node", "local"), None)
    whole_gather = mesh.shape["node"] == 2 * Z_COUNT and mesh.shape["local"] == 4
    return jax.shard_map(
        block_device if whole_gather else exchange_device,
        mesh=mesh,
        in_specs=in_specs,
        out_specs=out_specs,
        check_vma=False,
    )
```
